32 devices in a mesh: nodes: 4 (over x, core), batch: 8 (over z, y).
Axes of the slice: x: 2, y: 2, z: 4, core: 2. Of those that a mesh axis runs over, the one named last changes fastest.
Arguments:
- leaves: float32 [8, 128, 1024], P('nodes', None, 'batch'), may hold values from -340 to 8
- prod_child: int32 [8, 2], replicated, may hold values from 0 to 7
- block_weight: float32 [512, 128, 128], P('nodes'), may hold values from 0.0001 to 0.01
- block_child: int32 [4, 128], P('nodes'), may hold values from 0 to 7
- block_parent: int32 [4, 128], P('nodes'), may hold values from 0 to 3, as said below
- block_count: int32 [4], P('nodes'), may hold values from 32 to 128, as said below
- upper_flow: float32 [16, 128, 1024], P('nodes', None, 'batch'), may hold values from 0.1 to 1
Outputs:
- sum_values: float32 [16, 128, 1024], P('nodes', None, 'batch')
- leaf_flow: float32 [8, 128, 1024], P('nodes', None, 'batch')
- param_flow: float32 [512, 128, 128], P(('nodes', 'batch'))
The draws below stay inside these ranges and needn't reach their ends.
Inputs may be any that keep to these rules, and one draw needn't show every extreme that they name: `block_parent`: every owner's first 4 slots name its sum groups 0 to 3 in order. `block_count`: some owner has all 128 slots live.
All inputs are finite; a program needn't handle non-finite values.
Results may differ from the reference program's by a relative error of at most 0.0003.
Values sent between devices are 32-bit elements; how exact they have to be, the bound alone decides.
A program may use at most 128 MiB of HBM per device.

```python
import math
import jax
import jax.numpy as jnp
from jax import lax

G = 128
QD = 4
BPO = 128
NG = 8
PG = 8
QG = 16
NB = 512
SAMPLES = 1024
N_NODES = 4


def draw_leaves(key, part):
    base_key = jax.random.fold_in(key, 11)
    shift_key = jax.random.fold_in(key, 12)
    base = jnp.clip(jax.random.normal(base_key, (NG, G, SAMPLES), jnp.float32), -6.0, 6.0)
    offset = jax.random.uniform(shift_key, (1, 1, SAMPLES), jnp.float32, -4.0, 0.0)
    return base - 2.0 + offset


def draw_block_parent(key, part):
    slots = jnp.arange(BPO, dtype=jnp.int32)[None, :]
    picked = jax.random.randint(jax.random.fold_in(key, 21), (N_NODES, BPO), 0, QD)
    return jnp.where(slots < QD, slots, picked).astype(jnp.int32)


def draw_block_count(key, part):
    counts = jax.random.randint(jax.random.fold_in(key, 31), (N_NODES,), BPO // 4, BPO + 1)
    fullest = jax.random.randint(jax.random.fold_in(key, 32), (), 0, N_NODES)
    return jnp.where(jnp.arange(N_NODES, dtype=jnp.int32) == fullest, BPO, counts).astype(jnp.int32)


def set_ends(entries, key, smallest, high):
    dims = entries.shape
    place = [jax.random.randint(jax.random.fold_in(key, axis), (), 0, dims[axis]) for axis in range(len(dims))]
    entries = entries.at[tuple(place)].set(smallest)
    longest = dims.index(max(dims))
    place[longest] = (place[longest] + 1) % dims[longest]
    return entries.at[tuple(place)].set(high)


def level_of(rng, shape, cuts, least, top_value):
    factor_of, own = 1.0, jax.random.fold_in(rng, 6)
    for axis_at, parts in cuts:
        steps = jnp.exp(jax.random.uniform(jax.random.fold_in(own, axis_at), (parts,), jnp.float32, least / len(cuts), top_value / len(cuts)))
        factor_of = factor_of * jnp.repeat(steps, shape[axis_at] // parts).reshape([-1 if axis == axis_at else 1 for axis in range(len(shape))])
    return factor_of


def setup_inputs(seed: int = 0) -> dict:
    arg_keys = jax.random.split(jax.random.key(seed), 8)
    leaves = draw_leaves(jax.random.fold_in(arg_keys[7], 71), 0)
    prod_child = set_ends(jax.random.randint(arg_keys[1], (PG, 2), 0, NG), jax.random.fold_in(arg_keys[1], 1), 0, NG - 1).astype(jnp.int32)
    block_weight = jnp.clip(jnp.exp(math.log(0.01) - 4.6051702 * jax.random.uniform(arg_keys[2], (NB, G, G), jnp.float32) ** level_of(arg_keys[2], (NB, G, G), ((0, 4),), -0.2, 0.2)), 0.0001, 0.01)
    block_child = set_ends(jax.random.randint(arg_keys[3], (N_NODES, BPO), 0, PG), jax.random.fold_in(arg_keys[3], 1), 0, PG - 1).astype(jnp.int32)
    block_parent = draw_block_parent(jax.random.fold_in(arg_keys[7], 71), 0)
    block_count = draw_block_count(jax.random.fold_in(arg_keys[7], 71), 0)
    upper_flow = jnp.clip(jnp.exp(math.log(1.0) - 2.3025851 * jax.random.uniform(arg_keys[6], (QG, G, SAMPLES), jnp.float32) ** level_of(arg_keys[6], (QG, G, SAMPLES), ((0, 4), (2, 8)), -0.2, 0.2)), 0.1, 1.0)
    return dict(leaves=leaves, prod_child=prod_child, block_weight=block_weight, block_child=block_child, block_parent=block_parent, block_count=block_count, upper_flow=upper_flow)


very_low = -1e30


def reference(leaves, prod_child, block_weight, block_child, block_parent, block_count, upper_flow):
    high = lax.Precision.HIGHEST
    products = leaves[prod_child[:, 0]] + leaves[prod_child[:, 1]]
    peak = jnp.max(products, axis=1)
    owners = block_child.shape[0]
    per_owner = block_child.shape[1]
    groups_each = upper_flow.shape[0] // owners
    child = block_child.reshape(-1)
    parent = (block_parent + (jnp.arange(owners, dtype=jnp.int32) * groups_each)[:, None]).reshape(-1)
    live = (jnp.arange(per_owner, dtype=jnp.int32)[None, :] < block_count[:, None]).reshape(-1)
    top = jax.ops.segment_max(jnp.where(live[:, None], peak[child], very_low), parent, num_segments=upper_flow.shape[0])

    def shifted_of(c, q, l):
        return jnp.exp(jnp.where(l, products[c] - top[q][None, :], very_low))

    def forward(total, item):
        c, q, l, w = item
        sh = shifted_of(c, q, l)
        return total.at[q].add(jnp.dot(w, sh, precision=high, preferred_element_type=jnp.float32)), None

    total = lax.scan(forward, jnp.zeros(upper_flow.shape, jnp.float32), (child, parent, live, block_weight))[0]
    sum_values = top[:, None, :] + jnp.log(total)
    factor = upper_flow / total

    def backward(flows, item):
        c, q, l, w = item
        sh = shifted_of(c, q, l)
        par = factor[q]
        back = jnp.dot(w.T, par, precision=high, preferred_element_type=jnp.float32)
        flows = flows.at[c].add(sh * back)
        weight_flow = w * jnp.dot(par, sh.T, precision=high, preferred_element_type=jnp.float32)
        return flows, weight_flow

    product_flow, param_flow = lax.scan(backward, jnp.zeros(products.shape, jnp.float32), (child, parent, live, block_weight))
    leaf_flow = jnp.zeros(leaves.shape, jnp.float32).at[prod_child[:, 0]].add(product_flow)
    leaf_flow = leaf_flow.at[prod_child[:, 1]].add(product_flow)
    return sum_values, leaf_flow, param_flow
```

```python
import jax
import jax.numpy as jnp
from jax import lax
from jax.sharding import PartitionSpec as P

very_low = -1e30
high = lax.Precision.HIGH


def body(leaves, prod_child, block_weight, block_child, block_parent, block_count, upper_flow):
    total_prod = prod_child.shape[0]
    sum_each = upper_flow.shape[0]
    blocks = block_weight.shape[0]
    keep = blocks // lax.axis_size("batch")
    every = lax.all_gather(leaves, "nodes", axis=0, tiled=True)
    select = jax.nn.one_hot(prod_child[:, 0], every.shape[0], dtype=jnp.float32) + jax.nn.one_hot(
        prod_child[:, 1], every.shape[0], dtype=jnp.float32
    )
    products = every[prod_child[:, 0]] + every[prod_child[:, 1]]
    peak = jnp.max(products, axis=1)
    child = block_child.reshape(-1)
    parent = block_parent.reshape(-1)
    live = jnp.arange(blocks, dtype=jnp.int32) < block_count[0]
    pair = parent * total_prod + child
    pairs = sum_each * total_prod
    hot = jnp.where(live[:, None], jax.nn.one_hot(pair, pairs, dtype=jnp.float32), 0.0)
    weight = jnp.einsum(
        "bp,bij->pij", hot, block_weight, precision=high, preferred_element_type=jnp.float32
    ).reshape(sum_each, total_prod, *block_weight.shape[1:])
    has = (jnp.max(hot, axis=0) > 0.0).reshape(sum_each, total_prod)[:, :, None]
    top = jnp.max(jnp.where(has, peak[None], very_low), axis=1)
    scale = jnp.where(has, jnp.exp(jnp.where(has, peak[None] - top[:, None], 0.0)), 0.0)
    unit = jnp.exp(products - peak[:, None])
    total = jnp.einsum(
        "qcij,qcjs->qis",
        weight,
        unit[None] * scale[:, :, None],
        precision=high,
        preferred_element_type=jnp.float32,
    )
    sum_values = top[:, None, :] + jnp.log(total)
    factor = upper_flow / total
    scaled = factor[:, None] * scale[:, :, None]
    outer = jnp.einsum(
        "qcis,cjs->qcij", scaled, unit, precision=high, preferred_element_type=jnp.float32
    )
    outer = lax.psum(outer.reshape(pairs, *block_weight.shape[1:]), "batch")
    back = jnp.einsum(
        "qcij,qcis->cjs", weight, scaled, precision=high, preferred_element_type=jnp.float32
    )
    leaf_flow = lax.psum_scatter(
        jnp.einsum(
            "cg,cjs->gjs",
            select,
            unit * back,
            precision=lax.Precision.HIGHEST,
            preferred_element_type=jnp.float32,
        ),
        "nodes",
        scatter_dimension=0,
        tiled=True,
    )
    first = lax.axis_index("batch") * keep
    own = lax.dynamic_slice_in_dim(block_weight, first, keep, 0)
    own_pair = lax.dynamic_slice_in_dim(pair, first, keep, 0)
    own_live = lax.dynamic_slice_in_dim(live, first, keep, 0)
    param_flow = jnp.where(own_live[:, None, None], own * outer[own_pair], 0.0)
    return (sum_values, leaf_flow, param_flow)


def solution(mesh):
    placed = (
        P("nodes", None, "batch"),
        P(),
        P("nodes", None, None),
        P("nodes", None),
        P("nodes", None),
        P("nodes"),
        P("nodes", None, "batch"),
    )
    return jax.shard_map(
        body,
        mesh=mesh,
        in_specs=placed,
        out_specs=(
            P("nodes", None, "batch"),
            P("nodes", None, "batch"),
            P(("nodes", "batch"), None, None),
        ),
        check_vma=False,
    )
```

```python
import jax
import jax.numpy as jnp
from jax import lax
from jax.experimental import pallas as pl
from jax.experimental.pallas import tpu as pltpu
from jax.sharding import PartitionSpec as P

very_low = -1e30
high = lax.Precision.HIGH


def body(leaves, prod_child, block_weight, block_child, block_parent, block_count, upper_flow):
    total_prod = prod_child.shape[0]
    sum_each = upper_flow.shape[0]
    blocks = block_weight.shape[0]
    keep = blocks // lax.axis_size("batch")
    every = lax.all_gather(leaves, "nodes", axis=0, tiled=True)
    select = jax.nn.one_hot(prod_child[:, 0], every.shape[0], dtype=jnp.float32) + jax.nn.one_hot(
        prod_child[:, 1], every.shape[0], dtype=jnp.float32
    )
    products = every[prod_child[:, 0]] + every[prod_child[:, 1]]
    peak = jnp.max(products, axis=1)
    child = block_child.reshape(-1)
    parent = block_parent.reshape(-1)
    live = jnp.arange(blocks, dtype=jnp.int32) < block_count[0]
    pair = parent * total_prod + child
    pairs = sum_each * total_prod
    hot = jnp.where(live[:, None], jax.nn.one_hot(pair, pairs, dtype=jnp.float32), 0.0)
    weight = jnp.einsum(
        "bp,bij->pij", hot, block_weight, precision=high, preferred_element_type=jnp.float32
    ).reshape(sum_each, total_prod, *block_weight.shape[1:])
    has = (jnp.max(hot, axis=0) > 0.0).reshape(sum_each, total_prod)[:, :, None]
    top = jnp.max(jnp.where(has, peak[None], very_low), axis=1)
    scale = jnp.where(has, jnp.exp(jnp.where(has, peak[None] - top[:, None], 0.0)), 0.0)
    unit = jnp.exp(products - peak[:, None])
    total = jnp.einsum(
        "qcij,qcjs->qis",
        weight,
        unit[None] * scale[:, :, None],
        precision=high,
        preferred_element_type=jnp.float32,
    )
    sum_values = top[:, None, :] + jnp.log(total)
    factor = upper_flow / total
    scaled = factor[:, None] * scale[:, :, None]
    outer = jnp.einsum(
        "qcis,cjs->qcij", scaled, unit, precision=high, preferred_element_type=jnp.float32
    )
    outer = lax.psum(outer.reshape(pairs, *block_weight.shape[1:]), "batch")
    back = jnp.einsum(
        "qcij,qcis->cjs", weight, scaled, precision=high, preferred_element_type=jnp.float32
    )
    leaf_flow = lax.psum_scatter(
        jnp.einsum(
            "cg,cjs->gjs",
            select,
            unit * back,
            precision=lax.Precision.HIGHEST,
            preferred_element_type=jnp.float32,
        ),
        "nodes",
        scatter_dimension=0,
        tiled=True,
    )
    first = lax.axis_index("batch") * keep
    own = lax.dynamic_slice_in_dim(block_weight, first, keep, 0)
    own_pair = lax.dynamic_slice_in_dim(pair, first, keep, 0)
    own_live = lax.dynamic_slice_in_dim(live, first, keep, 0)
    param_flow = jnp.where(own_live[:, None, None], own * outer[own_pair], 0.0)
    return (sum_values, leaf_flow, param_flow)


MESH = pl.DeviceIdType.MESH
f32, bf16 = jnp.float32, jnp.bfloat16


def split(value):
    top_part = value.astype(bf16)
    return top_part, (value - top_part.astype(f32)).astype(bf16)


def dot3(a, b, dims):
    (a_hi, a_lo), (b_hi, b_lo) = a, b
    dot = lambda p, q: lax.dot_general(p, q, (dims, ((), ())), preferred_element_type=f32)
    return dot(a_hi, b_hi) + dot(a_hi, b_lo) + dot(a_lo, b_hi)


def weight_kernel(pair_ref, count_ref, w_ref, hi_ref, lo_ref, acc):
    step = pl.program_id(0)
    size = w_ref.shape[0]

    @pl.when(step == 0)
    def _():
        acc[...] = jnp.zeros_like(acc)

    def add(b, carry):
        at = pair_ref[step * size + b]
        acc[at] = acc[at] + w_ref[b]
        return carry

    lax.fori_loop(0, jnp.clip(count_ref[0] - step * size, 0, size), add, 0)

    @pl.when(step == pl.num_programs(0) - 1)
    def _():
        def out(p, carry):
            hi_ref[p], lo_ref[p] = split(acc[p])
            return carry

        lax.fori_loop(0, acc.shape[0], out, 0)


def sum_weights(block_weight, pair, count, pairs):
    blocks, rows, columns = block_weight.shape
    size = 16
    whole = pl.BlockSpec((pairs, rows, columns), lambda i, *_: (0, 0, 0))
    return pl.pallas_call(
        weight_kernel,
        grid_spec=pltpu.PrefetchScalarGridSpec(
            num_scalar_prefetch=2,
            grid=(blocks // size,),
            in_specs=[pl.BlockSpec((size, rows, columns), lambda i, *_: (i, 0, 0))],
            out_specs=[whole, whole],
            scratch_shapes=[pltpu.VMEM((pairs, rows, columns), f32)],
        ),
        out_shape=[jax.ShapeDtypeStruct((pairs, rows, columns), bf16)] * 2,
        compiler_params=pltpu.CompilerParams(vmem_limit_bytes=24 << 20),
    )(pair, count, block_weight)


def main_kernel(
    child_of, pair_of, alive, select, leaves, w_hi, w_lo, mask, upper, own_weight,
    sum_values, leaf_flow, param_flow,
    L, F, cur, fcur, u_hi, u_lo, peaks, scale, total, outer, part, got_core, mid, got_x,
    recv_l, send_lx, send_lc, send_ly, send_lz, recv_f, send_fy, send_fz, send_core, recv_core, send_x, recv_x,
):
    n, t = lax.axis_index("nodes"), lax.axis_index("batch")
    x, k, z, y = n // 2, n % 2, t // 2, t % 2
    depth = 4
    nx, nc, nxc = (1 - x) * 2 + k, x * 2 + 1 - k, (1 - x) * 2 + 1 - k
    by_x, by_core, by_y = (nx, t), (nc, t), (n, z * 2 + 1 - y)
    by_z = ((n, t - 2), (n, t + 2))
    has_z = (z > 0, z < depth - 1)
    prods, sums = u_hi.shape[0], upper.shape[0]
    wide = upper.shape[1]
    keep = outer.shape[0]
    very = f32(very_low)

    L[t * 4 + n] = leaves[...]
    barrier = pltpu.get_barrier_semaphore()
    for partner in (by_x, by_core, by_y):
        pl.semaphore_signal(barrier, inc=1, device_id=partner, device_id_type=MESH)
    for side in range(2):
        @pl.when(has_z[side])
        def _():
            pl.semaphore_signal(barrier, inc=1, device_id=by_z[side], device_id_type=MESH)
    pl.semaphore_wait(barrier, 3 + (z > 0).astype(jnp.int32) + (z < depth - 1).astype(jnp.int32))

    def remote(src, dst, send, recv, to):
        return pltpu.make_async_remote_copy(
            src_ref=src, dst_ref=dst, send_sem=send, recv_sem=recv, device_id=to, device_id_type=MESH
        )

    def leaf_to(nn, tt, send, to):
        at = L.at[tt * 4 + nn]
        return remote(at, at, send, recv_l.at[tt * 4 + nn], to)

    def leaf_x(tt):
        return leaf_to(n, tt, send_lx.at[tt], by_x)

    def leaf_c(nn, which, tt):
        return leaf_to(nn, tt, send_lc.at[which * 8 + tt], by_core)

    def leaf_y(zz):
        return leaf_to(n, zz * 2 + y, send_ly.at[zz], by_y)

    def leaf_z(zz, side):
        return leaf_to(n, zz * 2 + y, send_lz.at[side * depth + zz], by_z[side])

    def flow_to(tt, send, to):
        at = F.at[tt]
        return remote(at, at, send, recv_f.at[tt], to)

    def flow_y(zz):
        return flow_to(zz * 2 + y, send_fy.at[zz], by_y)

    def flow_z(zz, side):
        return flow_to(zz * 2 + y, send_fz.at[side * depth + zz], by_z[side])

    def arrived_l(nn, tt):
        leaf_to(nn, tt, send_lx.at[tt], by_x).wait_recv()

    def arrived_f(tt):
        flow_to(tt, send_fy.at[0], by_y).wait_recv()

    def spread(tt):
        leaf_x(tt).start()
        leaf_c(n, 0, tt).start()

    def gather(tt):
        arrived_l(nx, tt)
        leaf_c(nx, 1, tt).start()
        arrived_l(nc, tt)
        arrived_l(nxc, tt)

    def units(tt):
        cur[...] = L[pl.ds(tt * 4, 4)].reshape(cur.shape)

        def one(c, carry):
            prod = cur[child_of[2 * c]] + cur[child_of[2 * c + 1]]
            peak = jnp.max(prod, axis=0, keepdims=True)
            peaks[c] = peak
            u_hi[c], u_lo[c] = split(jnp.exp(prod - peak))
            return carry

        lax.fori_loop(0, prods, one, 0)
        tops = []
        for q in range(sums):
            on = mask[q] > 0.0
            top = jnp.max(jnp.where(on, peaks[...], very), axis=0, keepdims=True)
            scale[q] = jnp.where(on, jnp.exp(jnp.where(on, peaks[...] - top, 0.0)), 0.0)
            tops.append(top[0])
        return tops

    def outers(tt, first):
        fcur[...] = F[tt]

        def one(b, carry):
            q, c = pair_of[2 * (t * keep + b)], pair_of[2 * (t * keep + b) + 1]
            f = split(fcur[q] * scale[q, c])
            value = dot3(f, (u_hi[c], u_lo[c]), ((1,), (1,)))
            outer[b] = value if first else outer[b] + value
            return carry

        lax.fori_loop(0, keep, one, 0)

    leaf_x(t).start()
    leaf_c(n, 0, t).start()
    for side in range(2):
        @pl.when(has_z[side])
        def _():
            leaf_z(z, side).start()
    leaf_y(z).start()
    gather(t)
    tops = units(t)
    total[...] = jnp.zeros_like(total)

    def ahead(c, carry):
        value = dot3((w_hi[c], w_lo[c]), (u_hi[c], u_lo[c]), ((1,), (0,)))
        for q in range(sums):
            rows = pl.ds(q * wide, wide)
            total[rows] += value[q * wide : (q + 1) * wide] * scale[q, c]
        return carry

    lax.fori_loop(0, prods, ahead, 0)
    for q in range(sums):
        tot = total[pl.ds(q * wide, wide)]
        sum_values[q] = tops[q] + jnp.log(tot)
        F[t, q] = upper[q] / tot
    for side in range(2):
        @pl.when(has_z[side])
        def _():
            flow_z(z, side).start()
    flow_y(z).start()

    part[...] = jnp.zeros_like(part)

    def behind(c, carry):
        f = jnp.concatenate([F[t, q] * scale[q, c] for q in range(sums)], axis=0)
        value = dot3((w_hi[c], w_lo[c]), split(f), ((0,), (0,)))
        value = value * (u_hi[c].astype(f32) + u_lo[c].astype(f32))
        for g in range(part.shape[0]):
            part[g] += value * select[c * part.shape[0] + g]
        return carry

    lax.fori_loop(0, prods, behind, 0)

    def core_copy(xx):
        return remote(
            part.at[pl.ds(2 * (xx * 2 + 1 - k), 2)], got_core.at[xx], send_core.at[xx], recv_core.at[xx], by_core
        )

    for xx in range(2):
        core_copy(xx).start()

    outers(t, True)
    for xx in range(2):
        core_copy(xx).wait_recv()
        mid[xx] = part[pl.ds(2 * (xx * 2 + k), 2)] + got_core[xx]
    x_copy = remote(mid.at[1 - x], got_x, send_x, recv_x, by_x)
    x_copy.start()

    def other(zz):
        tt = zz * 2 + 1 - y
        arrived_l(n, tt)
        spread(tt)
        gather(tt)
        arrived_f(tt)
        units(tt)
        outers(tt, False)

    other(z)

    def hop(step, carry):
        places = (z - step, z + step)
        exists = (z - step >= 0, z + step < depth)
        for side in range(2):
            zz = places[side]
            @pl.when(exists[side])
            def _():
                tt = zz * 2 + y
                arrived_l(n, tt)
                spread(tt)
                leaf_y(zz).start()
                @pl.when(has_z[1 - side])
                def _():
                    leaf_z(zz, 1 - side).start()
                arrived_f(tt)
                flow_y(zz).start()
                @pl.when(has_z[1 - side])
                def _():
                    flow_z(zz, 1 - side).start()
        for side in range(2):
            zz = places[side]
            @pl.when(exists[side])
            def _():
                tt = zz * 2 + y
                gather(tt)
                units(tt)
                outers(tt, False)
                other(zz)
        return carry

    lax.fori_loop(1, depth, hop, 0)

    x_copy.wait_recv()
    leaf_flow[...] = mid[x] + got_x[...]

    def finish(b, carry):
        param_flow[b] = own_weight[b] * outer[b] * alive[t * keep + b]
        return carry

    lax.fori_loop(0, keep, finish, 0)

    for xx in range(2):
        core_copy(xx).wait_send()
    x_copy.wait_send()

    def sent(tt, carry):
        leaf_x(tt).wait_send()
        leaf_c(n, 0, tt).wait_send()
        leaf_c(nx, 1, tt).wait_send()
        return carry

    lax.fori_loop(0, 2 * depth, sent, 0)

    def sent_z(zz, carry):
        leaf_y(zz).wait_send()
        flow_y(zz).wait_send()
        @pl.when((zz >= z) & has_z[0])
        def _():
            leaf_z(zz, 0).wait_send()
            flow_z(zz, 0).wait_send()
        @pl.when((zz <= z) & has_z[1])
        def _():
            leaf_z(zz, 1).wait_send()
            flow_z(zz, 1).wait_send()
        return carry

    lax.fori_loop(0, depth, sent_z, 0)


def fused(leaves, prod_child, block_weight, block_child, block_parent, block_count, upper_flow):
    group, wide, samples = leaves.shape
    prods, sums = prod_child.shape[0], upper_flow.shape[0]
    blocks = block_weight.shape[0]
    owners, batches = lax.axis_size("nodes"), lax.axis_size("batch")
    keep = blocks // batches
    child, parent = block_child.reshape(-1), block_parent.reshape(-1)
    live = jnp.arange(blocks, dtype=jnp.int32) < block_count[0]
    w_hi, w_lo = sum_weights(block_weight, child * sums + parent, block_count, prods * sums)
    w_hi = w_hi.reshape(prods, sums * wide, wide)
    w_lo = w_lo.reshape(prods, sums * wide, wide)
    hit = live[:, None] & (
        (parent * prods + child)[:, None] == jnp.arange(sums * prods, dtype=jnp.int32)[None]
    )
    mask = jnp.max(hit.astype(f32), axis=0).reshape(sums, prods, 1, 1)
    mask = jnp.broadcast_to(mask, (sums, prods, 1, samples))
    select = (
        jax.nn.one_hot(prod_child[:, 0], owners * group, dtype=f32)
        + jax.nn.one_hot(prod_child[:, 1], owners * group, dtype=f32)
    ).reshape(-1)
    own = lax.dynamic_slice_in_dim(block_weight, lax.axis_index("batch") * keep, keep, 0)
    pair_of = jnp.stack([parent, child], axis=1).reshape(-1)
    smem, vmem = pl.BlockSpec(memory_space=pltpu.SMEM), pl.BlockSpec(memory_space=pltpu.VMEM)
    dma = lambda *dims: pltpu.SemaphoreType.DMA(dims)
    tile = (wide, samples)
    return pl.pallas_call(
        main_kernel,
        in_specs=[smem] * 4 + [vmem] * 6,
        out_specs=[vmem] * 3,
        out_shape=[
            jax.ShapeDtypeStruct(upper_flow.shape, f32),
            jax.ShapeDtypeStruct(leaves.shape, f32),
            jax.ShapeDtypeStruct(own.shape, f32),
        ],
        scratch_shapes=[
            pltpu.VMEM((batches * owners, group, *tile), f32),
            pltpu.VMEM((batches, sums, *tile), f32),
            pltpu.VMEM((owners * group, *tile), f32),
            pltpu.VMEM((sums, *tile), f32),
            pltpu.VMEM((prods, *tile), bf16),
            pltpu.VMEM((prods, *tile), bf16),
            pltpu.VMEM((prods, 1, samples), f32),
            pltpu.VMEM((sums, prods, 1, samples), f32),
            pltpu.VMEM((sums * wide, samples), f32),
            pltpu.VMEM(own.shape, f32),
            pltpu.VMEM((owners * group, *tile), f32),
            pltpu.VMEM((2, group, *tile), f32),
            pltpu.VMEM((2, group, *tile), f32),
            pltpu.VMEM((group, *tile), f32),
            dma(batches * owners),
            dma(batches),
            dma(2 * batches),
            dma(batches // 2),
            dma(batches),
            dma(batches),
            dma(batches // 2),
            dma(batches),
            dma(2),
            dma(2),
            pltpu.SemaphoreType.DMA,
            pltpu.SemaphoreType.DMA,
        ],
        compiler_params=pltpu.CompilerParams(
            collective_id=0, has_side_effects=True, vmem_limit_bytes=32 << 20
        ),
    )(
        prod_child.reshape(-1), pair_of, live.astype(f32), select,
        leaves, w_hi, w_lo, mask, upper_flow, own,
    )


def solution(mesh):
    placed = (
        P("nodes", None, "batch"),
        P(),
        P("nodes", None, None),
        P("nodes", None),
        P("nodes", None),
        P("nodes"),
        P("nodes", None, "batch"),
    )
    small = dict(mesh.shape) == {"nodes": 4, "batch": 8}
    return jax.shard_map(
        fused if small else body,
        mesh=mesh,
        in_specs=placed,
        out_specs=(
            P("nodes", None, "batch"),
            P("nodes", None, "batch"),
            P(("nodes", "batch"), None, None),
        ),
        check_vma=False,
    )
```

```python
import jax
import jax.numpy as jnp
from jax import lax
from jax.experimental import pallas as pl
from jax.experimental.pallas import tpu as pltpu
from jax.sharding import PartitionSpec as P

very_low = -1e30
high = lax.Precision.HIGH


def body(leaves, prod_child, block_weight, block_child, block_parent, block_count, upper_flow):
    total_prod = prod_child.shape[0]
    sum_each = upper_flow.shape[0]
    blocks = block_weight.shape[0]
    keep = blocks // lax.axis_size("batch")
    every = lax.all_gather(leaves, "nodes", axis=0, tiled=True)
    select = jax.nn.one_hot(prod_child[:, 0], every.shape[0], dtype=jnp.float32) + jax.nn.one_hot(
        prod_child[:, 1], every.shape[0], dtype=jnp.float32
    )
    products = every[prod_child[:, 0]] + every[prod_child[:, 1]]
    peak = jnp.max(products, axis=1)
    child = block_child.reshape(-1)
    parent = block_parent.reshape(-1)
    live = jnp.arange(blocks, dtype=jnp.int32) < block_count[0]
    pair = parent * total_prod + child
    pairs = sum_each * total_prod
    hot = jnp.where(live[:, None], jax.nn.one_hot(pair, pairs, dtype=jnp.float32), 0.0)
    weight = jnp.einsum(
        "bp,bij->pij", hot, block_weight, precision=high, preferred_element_type=jnp.float32
    ).reshape(sum_each, total_prod, *block_weight.shape[1:])
    has = (jnp.max(hot, axis=0) > 0.0).reshape(sum_each, total_prod)[:, :, None]
    top = jnp.max(jnp.where(has, peak[None], very_low), axis=1)
    scale = jnp.where(has, jnp.exp(jnp.where(has, peak[None] - top[:, None], 0.0)), 0.0)
    unit = jnp.exp(products - peak[:, None])
    total = jnp.einsum(
        "qcij,qcjs->qis",
        weight,
        unit[None] * scale[:, :, None],
        precision=high,
        preferred_element_type=jnp.float32,
    )
    sum_values = top[:, None, :] + jnp.log(total)
    factor = upper_flow / total
    scaled = factor[:, None] * scale[:, :, None]
    outer = jnp.einsum(
        "qcis,cjs->qcij", scaled, unit, precision=high, preferred_element_type=jnp.float32
    )
    outer = lax.psum(outer.reshape(pairs, *block_weight.shape[1:]), "batch")
    back = jnp.einsum(
        "qcij,qcis->cjs", weight, scaled, precision=high, preferred_element_type=jnp.float32
    )
    leaf_flow = lax.psum_scatter(
        jnp.einsum(
            "cg,cjs->gjs",
            select,
            unit * back,
            precision=lax.Precision.HIGHEST,
            preferred_element_type=jnp.float32,
        ),
        "nodes",
        scatter_dimension=0,
        tiled=True,
    )
    first = lax.axis_index("batch") * keep
    own = lax.dynamic_slice_in_dim(block_weight, first, keep, 0)
    own_pair = lax.dynamic_slice_in_dim(pair, first, keep, 0)
    own_live = lax.dynamic_slice_in_dim(live, first, keep, 0)
    param_flow = jnp.where(own_live[:, None, None], own * outer[own_pair], 0.0)
    return (sum_values, leaf_flow, param_flow)


MESH = pl.DeviceIdType.MESH
f32, bf16 = jnp.float32, jnp.bfloat16


def split(value):
    top_part = value.astype(bf16)
    return top_part, (value - top_part.astype(f32)).astype(bf16)


def dot3(a, b, dims):
    (a_hi, a_lo), (b_hi, b_lo) = a, b
    dot = lambda p, q: lax.dot_general(p, q, (dims, ((), ())), preferred_element_type=f32)
    return dot(a_hi, b_hi) + dot(a_hi, b_lo) + dot(a_lo, b_hi)


def weight_kernel(child_ref, parent_ref, count_ref, w_ref, hi_ref, lo_ref, mask_ref, acc):
    step = pl.program_id(0)
    size = w_ref.shape[0]
    sums = hi_ref.shape[0] // mask_ref.shape[1]

    @pl.when(step == 0)
    def _():
        acc[...] = jnp.zeros_like(acc)
        mask_ref[...] = jnp.zeros_like(mask_ref)

    def add(b, carry):
        c, q = child_ref[0, step * size + b], parent_ref[0, step * size + b]
        at = c * sums + q
        acc[at] = acc[at] + w_ref[b]
        mask_ref[q, c] = jnp.ones(mask_ref.shape[2:], f32)
        return carry

    lax.fori_loop(0, jnp.clip(count_ref[0] - step * size, 0, size), add, 0)

    @pl.when(step == pl.num_programs(0) - 1)
    def _():
        def out(p, carry):
            hi_ref[p], lo_ref[p] = split(acc[p])
            return carry

        lax.fori_loop(0, acc.shape[0], out, 0)


def sum_weights(block_weight, child, parent, count, sums, prods, samples):
    blocks, rows, columns = block_weight.shape
    size = 16
    pairs = sums * prods
    whole = pl.BlockSpec((pairs, rows, columns), lambda i, *_: (0, 0, 0))
    return pl.pallas_call(
        weight_kernel,
        grid_spec=pltpu.PrefetchScalarGridSpec(
            num_scalar_prefetch=3,
            grid=(blocks // size,),
            in_specs=[pl.BlockSpec((size, rows, columns), lambda i, *_: (i, 0, 0))],
            out_specs=[
                whole, whole, pl.BlockSpec((sums, prods, 1, samples), lambda i, *_: (0, 0, 0, 0))
            ],
            scratch_shapes=[pltpu.VMEM((pairs, rows, columns), f32)],
        ),
        out_shape=[jax.ShapeDtypeStruct((pairs, rows, columns), bf16)] * 2
        + [jax.ShapeDtypeStruct((sums, prods, 1, samples), f32)],
        compiler_params=pltpu.CompilerParams(vmem_limit_bytes=56 << 20),
    )(child, parent, count, block_weight)


def main_kernel(
    child_of, child, parent, count, leaves, w_hi, w_lo, mask, upper, weight,
    sum_values, leaf_flow, param_flow,
    L, F, cur, fcur, u_hi, u_lo, peaks, scale, cur_1, u_hi_1, u_lo_1, peaks_1, scale_1,
    total, outer, own_weight, part, got_core, mid, got_x,
    recv_l, send_lx, send_lc, send_ly, send_lz, recv_f, send_fy, send_fz, send_core, recv_core, send_x, recv_x, own_sem,
):
    n, t = lax.axis_index("nodes"), lax.axis_index("batch")
    x, k, z, y = n // 2, n % 2, t // 2, t % 2
    depth = 4
    nx, nc, nxc = (1 - x) * 2 + k, x * 2 + 1 - k, (1 - x) * 2 + 1 - k
    by_x, by_core, by_y = (nx, t), (nc, t), (n, z * 2 + 1 - y)
    by_z = ((n, t - 2), (n, t + 2))
    has_z = (z > 0, z < depth - 1)
    prods, sums = u_hi.shape[0], upper.shape[0]
    wide, samples = upper.shape[1:]
    keep = outer.shape[0]
    very = f32(very_low)

    own_copy = pltpu.make_async_copy(weight.at[pl.ds(t * keep, keep)], own_weight, own_sem)
    own_copy.start()
    L[t * 4 + n] = leaves[...]
    barrier = pltpu.get_barrier_semaphore()
    for partner in (by_x, by_core, by_y):
        pl.semaphore_signal(barrier, inc=1, device_id=partner, device_id_type=MESH)
    for side in range(2):
        @pl.when(has_z[side])
        def _():
            pl.semaphore_signal(barrier, inc=1, device_id=by_z[side], device_id_type=MESH)
    pl.semaphore_wait(barrier, 3 + (z > 0).astype(jnp.int32) + (z < depth - 1).astype(jnp.int32))

    def remote(src, dst, send, recv, to):
        return pltpu.make_async_remote_copy(
            src_ref=src, dst_ref=dst, send_sem=send, recv_sem=recv, device_id=to, device_id_type=MESH
        )

    def leaf_to(nn, tt, send, to):
        at = L.at[tt * 4 + nn]
        return remote(at, at, send, recv_l.at[tt * 4 + nn], to)

    def leaf_x(tt):
        return leaf_to(n, tt, send_lx.at[tt], by_x)

    def leaf_c(nn, which, tt):
        return leaf_to(nn, tt, send_lc.at[which * 8 + tt], by_core)

    def leaf_y(zz):
        return leaf_to(n, zz * 2 + y, send_ly.at[zz], by_y)

    def leaf_z(zz, side):
        return leaf_to(n, zz * 2 + y, send_lz.at[side * depth + zz], by_z[side])

    def flow_to(tt, send, to):
        at = F.at[tt]
        return remote(at, at, send, recv_f.at[tt], to)

    def flow_y(zz):
        return flow_to(zz * 2 + y, send_fy.at[zz], by_y)

    def flow_z(zz, side):
        return flow_to(zz * 2 + y, send_fz.at[side * depth + zz], by_z[side])

    def arrived_l(nn, tt):
        leaf_to(nn, tt, send_lx.at[tt], by_x).wait_recv()

    def arrived_f(tt):
        flow_to(tt, send_fy.at[0], by_y).wait_recv()

    def spread(tt):
        leaf_x(tt).start()
        leaf_c(n, 0, tt).start()

    def from_x(tt):
        arrived_l(nx, tt)
        leaf_c(nx, 1, tt).start()

    def from_core(tt):
        arrived_l(nc, tt)
        arrived_l(nxc, tt)

    def each_side(step, act):
        for side, zz, exists in ((0, z - step, z - step >= 0), (1, z + step, z + step < depth)):
            @pl.when(exists)
            def _():
                act(side, zz)

    def leaf_hop(side, zz):
        arrived_l(n, zz * 2 + y)
        @pl.when(has_z[1 - side])
        def _():
            leaf_z(zz, 1 - side).start()
        leaf_y(zz).start()
        spread(zz * 2 + y)

    def flow_hop(side, zz):
        arrived_f(zz * 2 + y)
        @pl.when(has_z[1 - side])
        def _():
            flow_z(zz, 1 - side).start()
        flow_y(zz).start()

    def leaf_turn(side, zz):
        arrived_l(n, zz * 2 + 1 - y)
        spread(zz * 2 + 1 - y)

    def both_x(side, zz):
        for yy in range(2):
            from_x(zz * 2 + yy)

    def units(cur, u_hi, u_lo, peaks, scale):
        times = cur.shape[-1] // samples

        def some(i, carry):
            for c in (2 * i, 2 * i + 1):
                prod = cur[child_of[c, 0]] + cur[child_of[c, 1]]
                peak = jnp.max(prod, axis=0, keepdims=True)
                peaks[c] = peak
                u_hi[c], u_lo[c] = split(jnp.exp(prod - peak))
            return carry

        lax.fori_loop(0, prods // 2, some, 0)
        tops = []
        for q in range(sums):
            on = jnp.concatenate([mask[q]] * times, axis=-1) > 0.0
            top = jnp.max(jnp.where(on, peaks[...], very), axis=0, keepdims=True)
            scale[q] = jnp.where(on, jnp.exp(jnp.where(on, peaks[...] - top, 0.0)), 0.0)
            tops.append(top[0])
        return tops

    def outers(zz):
        for yy in range(2):
            columns = pl.ds(yy * samples, samples)
            cur[:, :, columns] = L[pl.ds((zz * 2 + yy) * 4, 4)].reshape(cur_1.shape)
            fcur[:, :, columns] = F[zz * 2 + yy]
        units(cur, u_hi, u_lo, peaks, scale)

        def some(i, carry):
            for j in range(4):
                b = 4 * i + j
                q, c = parent[0, t * keep + b], child[0, t * keep + b]
                outer[b] += dot3(split(fcur[q] * scale[q, c]), (u_hi[c], u_lo[c]), ((1,), (1,)))
            return carry

        lax.fori_loop(0, keep // 4, some, 0)

    def at_hop(step):
        def one(side, carry):
            zz = z + step * (2 * side - 1)

            @pl.when((zz >= 0) & (zz < depth))
            def _():
                from_core(zz * 2)
                from_core(zz * 2 + 1)
                arrived_f(zz * 2 + 1 - y)
                outers(zz)
            return carry

        lax.fori_loop(0, 2, one, 0)

    spread(t)
    for side in range(2):
        @pl.when(has_z[side])
        def _():
            leaf_z(z, side).start()
    leaf_y(z).start()
    outer[...] = jnp.zeros_like(outer)
    total[...] = jnp.zeros_like(total)
    part[...] = jnp.zeros_like(part)
    from_x(t)
    from_core(t)
    cur_1[...] = L[pl.ds(t * 4, 4)].reshape(cur_1.shape)
    tops = units(cur_1, u_hi_1, u_lo_1, peaks_1, scale_1)

    def ahead(i, carry):
        for c in (2 * i, 2 * i + 1):
            value = dot3((w_hi[c], w_lo[c]), (u_hi_1[c], u_lo_1[c]), ((1,), (0,)))
            for q in range(sums):
                total[q * wide : (q + 1) * wide] += value[q * wide : (q + 1) * wide] * scale_1[q, c]
        return carry

    lax.fori_loop(0, prods // 2, ahead, 0)
    for q in range(sums):
        F[t, q] = upper[q] / total[q * wide : (q + 1) * wide]
    for side in range(2):
        @pl.when(has_z[side])
        def _():
            flow_z(z, side).start()
    flow_y(z).start()
    each_side(1, leaf_hop)
    leaf_turn(0, z)
    for q in range(sums):
        sum_values[q] = tops[q] + jnp.log(total[q * wide : (q + 1) * wide])

    def behind(c, carry):
        f = jnp.concatenate([F[t, q] * scale_1[q, c] for q in range(sums)], axis=0)
        value = dot3((w_hi[c], w_lo[c]), split(f), ((0,), (0,)))
        value = value * (u_hi_1[c].astype(f32) + u_lo_1[c].astype(f32))
        for g in range(part.shape[0]):
            times = (child_of[c, 0] == g).astype(f32) + (child_of[c, 1] == g).astype(f32)
            part[g] += value * times
        return carry

    lax.fori_loop(0, prods, behind, 0)

    def core_copy(xx):
        return remote(
            part.at[pl.ds(2 * (xx * 2 + 1 - k), 2)], got_core.at[xx], send_core.at[xx], recv_core.at[xx], by_core
        )

    for xx in range(2):
        core_copy(xx).start()
    each_side(2, leaf_hop)
    each_side(1, leaf_turn)
    each_side(1, flow_hop)
    from_x(z * 2 + 1 - y)
    for xx in range(2):
        core_copy(xx).wait_recv()
        mid[xx] = part[pl.ds(2 * (xx * 2 + k), 2)] + got_core[xx]
    x_copy = remote(mid.at[1 - x], got_x, send_x, recv_x, by_x)
    x_copy.start()

    from_core(z * 2 + 1 - y)
    arrived_f(z * 2 + 1 - y)
    outers(z)
    each_side(3, leaf_hop)
    each_side(2, leaf_turn)
    each_side(1, both_x)
    each_side(2, flow_hop)
    each_side(3, leaf_turn)
    each_side(2, both_x)
    at_hop(1)
    each_side(3, flow_hop)
    each_side(3, both_x)
    at_hop(2)
    at_hop(3)

    x_copy.wait_recv()
    leaf_flow[...] = mid[x] + got_x[...]
    own_copy.wait()

    def finish(b, carry):
        alive = (t * keep + b < count[0]).astype(f32)
        param_flow[b] = own_weight[b] * outer[b] * alive
        return carry

    lax.fori_loop(0, keep, finish, 0)

    for xx in range(2):
        core_copy(xx).wait_send()
    x_copy.wait_send()

    def sent(tt, carry):
        leaf_x(tt).wait_send()
        leaf_c(n, 0, tt).wait_send()
        leaf_c(nx, 1, tt).wait_send()
        return carry

    lax.fori_loop(0, 2 * depth, sent, 0)

    def sent_z(zz, carry):
        leaf_y(zz).wait_send()
        flow_y(zz).wait_send()
        @pl.when((zz >= z) & has_z[0])
        def _():
            leaf_z(zz, 0).wait_send()
            flow_z(zz, 0).wait_send()
        @pl.when((zz <= z) & has_z[1])
        def _():
            leaf_z(zz, 1).wait_send()
            flow_z(zz, 1).wait_send()
        return carry

    lax.fori_loop(0, depth, sent_z, 0)


def fused(leaves, prod_child, block_weight, block_child, block_parent, block_count, upper_flow):
    group, wide, samples = leaves.shape
    prods, sums = prod_child.shape[0], upper_flow.shape[0]
    owners, batches = lax.axis_size("nodes"), lax.axis_size("batch")
    keep = block_weight.shape[0] // batches
    w_hi, w_lo, mask = sum_weights(
        block_weight, block_child, block_parent, block_count, sums, prods, samples
    )
    w_hi = w_hi.reshape(prods, sums * wide, wide)
    w_lo = w_lo.reshape(prods, sums * wide, wide)
    smem, vmem = pl.BlockSpec(memory_space=pltpu.SMEM), pl.BlockSpec(memory_space=pltpu.VMEM)
    dma = lambda *dims: pltpu.SemaphoreType.DMA(dims)
    vec = lambda kind, *dims: pltpu.VMEM(dims, kind)
    two = 2 * samples
    return pl.pallas_call(
        main_kernel,
        in_specs=[smem] * 4 + [vmem] * 5 + [pl.BlockSpec(memory_space=pl.ANY)],
        out_specs=[vmem] * 3,
        out_shape=[
            jax.ShapeDtypeStruct(upper_flow.shape, f32),
            jax.ShapeDtypeStruct(leaves.shape, f32),
            jax.ShapeDtypeStruct((keep, *block_weight.shape[1:]), f32),
        ],
        scratch_shapes=[
            vec(f32, batches * owners, group, wide, samples),
            vec(f32, batches, sums, wide, samples),
            vec(f32, owners * group, wide, two),
            vec(f32, sums, wide, two),
            vec(bf16, prods, wide, two),
            vec(bf16, prods, wide, two),
            vec(f32, prods, 1, two),
            vec(f32, sums, prods, 1, two),
            vec(f32, owners * group, wide, samples),
            vec(bf16, prods, wide, samples),
            vec(bf16, prods, wide, samples),
            vec(f32, prods, 1, samples),
            vec(f32, sums, prods, 1, samples),
            vec(f32, sums * wide, samples),
            vec(f32, keep, *block_weight.shape[1:]),
            vec(f32, keep, *block_weight.shape[1:]),
            vec(f32, owners * group, wide, samples),
            vec(f32, 2, group, wide, samples),
            vec(f32, 2, group, wide, samples),
            vec(f32, group, wide, samples),
            dma(batches * owners),
            dma(batches),
            dma(2 * batches),
            dma(batches // 2),
            dma(batches),
            dma(batches),
            dma(batches // 2),
            dma(batches),
            dma(2),
            dma(2),
            pltpu.SemaphoreType.DMA,
            pltpu.SemaphoreType.DMA,
            pltpu.SemaphoreType.DMA,
        ],
        compiler_params=pltpu.CompilerParams(
            collective_id=0, has_side_effects=True, vmem_limit_bytes=56 << 20
        ),
    )(
        prod_child, block_child, block_parent, block_count,
        leaves, w_hi, w_lo, mask, upper_flow, block_weight,
    )


def solution(mesh):
    placed = (
        P("nodes", None, "batch"),
        P(),
        P("nodes", None, None),
        P("nodes", None),
        P("nodes", None),
        P("nodes"),
        P("nodes", None, "batch"),
    )
    small = dict(mesh.shape) == {"nodes": 4, "batch": 8}
    return jax.shard_map(
        fused if small else body,
        mesh=mesh,
        in_specs=placed,
        out_specs=(
            P("nodes", None, "batch"),
            P("nodes", None, "batch"),
            P(("nodes", "batch"), None, None),
        ),
        check_vma=False,
    )
```

```python
import functools

import jax
import jax.numpy as jnp
from jax import lax
from jax.experimental import pallas as pl
from jax.experimental.pallas import tpu as pltpu
from jax.sharding import PartitionSpec as P

very_low = -1e30
high = lax.Precision.HIGH


def body(leaves, prod_child, block_weight, block_child, block_parent, block_count, upper_flow):
    total_prod = prod_child.shape[0]
    sum_each = upper_flow.shape[0]
    blocks = block_weight.shape[0]
    keep = blocks // lax.axis_size("batch")
    every = lax.all_gather(leaves, "nodes", axis=0, tiled=True)
    select = jax.nn.one_hot(prod_child[:, 0], every.shape[0], dtype=jnp.float32) + jax.nn.one_hot(
        prod_child[:, 1], every.shape[0], dtype=jnp.float32
    )
    products = every[prod_child[:, 0]] + every[prod_child[:, 1]]
    peak = jnp.max(products, axis=1)
    child = block_child.reshape(-1)
    parent = block_parent.reshape(-1)
    live = jnp.arange(blocks, dtype=jnp.int32) < block_count[0]
    pair = parent * total_prod + child
    pairs = sum_each * total_prod
    hot = jnp.where(live[:, None], jax.nn.one_hot(pair, pairs, dtype=jnp.float32), 0.0)
    weight = jnp.einsum(
        "bp,bij->pij", hot, block_weight, precision=high, preferred_element_type=jnp.float32
    ).reshape(sum_each, total_prod, *block_weight.shape[1:])
    has = (jnp.max(hot, axis=0) > 0.0).reshape(sum_each, total_prod)[:, :, None]
    top = jnp.max(jnp.where(has, peak[None], very_low), axis=1)
    scale = jnp.where(has, jnp.exp(jnp.where(has, peak[None] - top[:, None], 0.0)), 0.0)
    unit = jnp.exp(products - peak[:, None])
    total = jnp.einsum(
        "qcij,qcjs->qis",
        weight,
        unit[None] * scale[:, :, None],
        precision=high,
        preferred_element_type=jnp.float32,
    )
    sum_values = top[:, None, :] + jnp.log(total)
    factor = upper_flow / total
    scaled = factor[:, None] * scale[:, :, None]
    outer = jnp.einsum(
        "qcis,cjs->qcij", scaled, unit, precision=high, preferred_element_type=jnp.float32
    )
    outer = lax.psum(outer.reshape(pairs, *block_weight.shape[1:]), "batch")
    back = jnp.einsum(
        "qcij,qcis->cjs", weight, scaled, precision=high, preferred_element_type=jnp.float32
    )
    leaf_flow = lax.psum_scatter(
        jnp.einsum(
            "cg,cjs->gjs",
            select,
            unit * back,
            precision=lax.Precision.HIGHEST,
            preferred_element_type=jnp.float32,
        ),
        "nodes",
        scatter_dimension=0,
        tiled=True,
    )
    first = lax.axis_index("batch") * keep
    own = lax.dynamic_slice_in_dim(block_weight, first, keep, 0)
    own_pair = lax.dynamic_slice_in_dim(pair, first, keep, 0)
    own_live = lax.dynamic_slice_in_dim(live, first, keep, 0)
    param_flow = jnp.where(own_live[:, None, None], own * outer[own_pair], 0.0)
    return (sum_values, leaf_flow, param_flow)


MESH = pl.DeviceIdType.MESH
f32, bf16 = jnp.float32, jnp.bfloat16


def split(value):
    top_part = value.astype(bf16)
    return top_part, (value - top_part.astype(f32)).astype(bf16)


def dot3(a, b, dims):
    (a_hi, a_lo), (b_hi, b_lo) = a, b
    dot = lambda p, q: lax.dot_general(p, q, (dims, ((), ())), preferred_element_type=f32)
    return dot(a_hi, b_hi) + dot(a_hi, b_lo) + dot(a_lo, b_hi)


def order_kernel(sums, count_ref, child_ref, parent_ref, whole_ref, real_ref):
    blocks = child_ref.shape[1]
    shape = (blocks, blocks)
    row = lax.broadcasted_iota(jnp.int32, shape, 0)
    column = lax.broadcasted_iota(jnp.int32, shape, 1)
    row_f, column_f = row.astype(f32), column.astype(f32)
    lane = lax.broadcasted_iota(jnp.int32, (1, blocks), 1)
    key = child_ref[...] * sums + parent_ref[...]
    key = jnp.where(lane < count_ref[0], key, 1 << 20).astype(f32)
    along = jnp.broadcast_to(key, shape)
    down = along.T
    before = (down < along) | ((down == along) & (row < column))
    rank = jnp.sum(before.astype(f32), axis=0, keepdims=True)
    rank_down = jnp.broadcast_to(rank, shape).T
    total = lambda take, value: jnp.sum(jnp.where(take, value, 0.0), axis=0, keepdims=True)
    here = rank_down == column_f
    order = total(here, row_f)
    same = total(here, down) == total(rank_down == column_f - 1.0, down)
    keep = jnp.where(same & (lane > 0), 1.0, 0.0)
    last = jnp.maximum(total(down <= column_f, jnp.ones(shape, f32)) - 1.0, 0.0)
    used = jnp.minimum(total(down == column_f, jnp.ones(shape, f32)), 1.0)
    whole_ref[0:1] = order.astype(jnp.int32)
    whole_ref[1:2] = last.astype(jnp.int32)
    real_ref[0:1] = keep
    real_ref[1:2] = used


def order_blocks(count, child, parent, sums):
    smem, vmem = pl.BlockSpec(memory_space=pltpu.SMEM), pl.BlockSpec(memory_space=pltpu.VMEM)
    return pl.pallas_call(
        functools.partial(order_kernel, sums),
        in_specs=[smem, vmem, vmem],
        out_specs=[vmem, vmem],
        out_shape=[
            jax.ShapeDtypeStruct((2, child.shape[1]), jnp.int32),
            jax.ShapeDtypeStruct((2, child.shape[1]), f32),
        ],
    )(count, child, parent)


def main_kernel(
    child_of, child, parent, count, whole, real, leaves, upper, weight,
    sum_values, leaf_flow, param_flow,
    L, F, cur, fcur, u_hi, u_lo, peaks, scale, cur_1, u_hi_1, u_lo_1, peaks_1, scale_1,
    total, outer, W, runs, w_hi, w_lo, part, got_core, mid, got_x,
    recv_l, send_lx, send_lc, send_ly, send_lz, recv_f, send_fy, send_fz, send_core, recv_core, send_x, recv_x, w_sem,
):
    n, t = lax.axis_index("nodes"), lax.axis_index("batch")
    x, k, z, y = n // 2, n % 2, t // 2, t % 2
    depth = 4
    nx, nc, nxc = (1 - x) * 2 + k, x * 2 + 1 - k, (1 - x) * 2 + 1 - k
    by_x, by_core, by_y = (nx, t), (nc, t), (n, z * 2 + 1 - y)
    by_z = ((n, t - 2), (n, t + 2))
    has_z = (z > 0, z < depth - 1)
    prods, sums = u_hi.shape[0], upper.shape[0]
    wide, samples = upper.shape[1:]
    keep = outer.shape[0]
    very = f32(very_low)

    blocks, pieces = W.shape[0], w_sem.shape[0]

    def weight_copy(i):
        at = pl.ds(i * (blocks // pieces), blocks // pieces)
        return pltpu.make_async_copy(weight.at[at], W.at[at], w_sem.at[i])

    for i in range(pieces):
        weight_copy(i).start()
    L[t * 4 + n] = leaves[...]
    barrier = pltpu.get_barrier_semaphore()
    for partner in (by_x, by_core, by_y):
        pl.semaphore_signal(barrier, inc=1, device_id=partner, device_id_type=MESH)
    for side in range(2):
        @pl.when(has_z[side])
        def _():
            pl.semaphore_signal(barrier, inc=1, device_id=by_z[side], device_id_type=MESH)
    pl.semaphore_wait(barrier, 3 + (z > 0).astype(jnp.int32) + (z < depth - 1).astype(jnp.int32))

    def remote(src, dst, send, recv, to):
        return pltpu.make_async_remote_copy(
            src_ref=src, dst_ref=dst, send_sem=send, recv_sem=recv, device_id=to, device_id_type=MESH
        )

    def leaf_to(nn, tt, send, to):
        at = L.at[tt * 4 + nn]
        return remote(at, at, send, recv_l.at[tt * 4 + nn], to)

    def leaf_x(tt):
        return leaf_to(n, tt, send_lx.at[tt], by_x)

    def leaf_c(nn, which, tt):
        return leaf_to(nn, tt, send_lc.at[which * 8 + tt], by_core)

    def leaf_y(zz):
        return leaf_to(n, zz * 2 + y, send_ly.at[zz], by_y)

    def leaf_z(zz, side):
        return leaf_to(n, zz * 2 + y, send_lz.at[side * depth + zz], by_z[side])

    def flow_to(tt, send, to):
        at = F.at[tt]
        return remote(at, at, send, recv_f.at[tt], to)

    def flow_y(zz):
        return flow_to(zz * 2 + y, send_fy.at[zz], by_y)

    def flow_z(zz, side):
        return flow_to(zz * 2 + y, send_fz.at[side * depth + zz], by_z[side])

    def arrived_l(nn, tt):
        leaf_to(nn, tt, send_lx.at[tt], by_x).wait_recv()

    def arrived_f(tt):
        flow_to(tt, send_fy.at[0], by_y).wait_recv()

    def spread(tt):
        leaf_x(tt).start()
        leaf_c(n, 0, tt).start()

    def from_x(tt):
        arrived_l(nx, tt)
        leaf_c(nx, 1, tt).start()

    def from_core(tt):
        arrived_l(nc, tt)
        arrived_l(nxc, tt)

    def each_side(step, act):
        for side, zz, exists in ((0, z - step, z - step >= 0), (1, z + step, z + step < depth)):
            @pl.when(exists)
            def _():
                act(side, zz)

    def leaf_hop(side, zz):
        arrived_l(n, zz * 2 + y)
        @pl.when(has_z[1 - side])
        def _():
            leaf_z(zz, 1 - side).start()
        leaf_y(zz).start()
        spread(zz * 2 + y)

    def flow_hop(side, zz):
        arrived_f(zz * 2 + y)
        @pl.when(has_z[1 - side])
        def _():
            flow_z(zz, 1 - side).start()
        flow_y(zz).start()

    def leaf_turn(side, zz):
        arrived_l(n, zz * 2 + 1 - y)
        spread(zz * 2 + 1 - y)

    def both_x(side, zz):
        for yy in range(2):
            from_x(zz * 2 + yy)

    def units(cur, u_hi, u_lo, peaks, scale):
        times = cur.shape[-1] // samples

        def some(i, carry):
            for c in (2 * i, 2 * i + 1):
                prod = cur[child_of[c, 0]] + cur[child_of[c, 1]]
                peak = jnp.max(prod, axis=0, keepdims=True)
                peaks[c] = peak
                u_hi[c], u_lo[c] = split(jnp.exp(prod - peak))
            return carry

        lax.fori_loop(0, prods // 2, some, 0)
        tops = []
        for q in range(sums):
            used = [real[1, c * sums + q] for c in range(prods)]
            top = peaks[0] + (used[0] - 1.0) * -very
            for c in range(1, prods):
                top = jnp.maximum(top, peaks[c] + (used[c] - 1.0) * -very)
            for c in range(prods):
                scale[q, c] = jnp.exp(jnp.minimum(peaks[c] - top, 0.0)) * used[c]
            tops.append(top)
        return tops

    def outers(zz):
        for yy in range(2):
            columns = pl.ds(yy * samples, samples)
            cur[:, :, columns] = L[pl.ds((zz * 2 + yy) * 4, 4)].reshape(cur_1.shape)
            fcur[:, :, columns] = F[zz * 2 + yy]
        units(cur, u_hi, u_lo, peaks, scale)

        def some(i, carry):
            for j in range(4):
                b = 4 * i + j
                q, c = parent[0, t * keep + b], child[0, t * keep + b]
                outer[b] += dot3(split(fcur[q] * scale[q, c]), (u_hi[c], u_lo[c]), ((1,), (1,)))
            return carry

        lax.fori_loop(0, keep // 4, some, 0)

    def at_hop(step):
        def one(side, carry):
            zz = z + step * (2 * side - 1)

            @pl.when((zz >= 0) & (zz < depth))
            def _():
                from_core(zz * 2)
                from_core(zz * 2 + 1)
                arrived_f(zz * 2 + 1 - y)
                outers(zz)
            return carry

        lax.fori_loop(0, 2, one, 0)

    spread(t)
    for side in range(2):
        @pl.when(has_z[side])
        def _():
            leaf_z(z, side).start()
    leaf_y(z).start()
    outer[...] = jnp.zeros_like(outer)
    total[...] = jnp.zeros_like(total)
    part[...] = jnp.zeros_like(part)

    for i in range(pieces):
        weight_copy(i).wait()

    def run(i, value):
        for j in range(4):
            at = 4 * i + j
            value = value * real[0, at] + W[whole[0, at]]
            runs[at] = value
        return value

    lax.fori_loop(0, blocks // 4, run, jnp.zeros(W.shape[1:], f32))
    from_x(t)

    def pick(c, carry):
        for q in range(sums):
            p = c * sums + q
            rows = pl.ds(q * wide, wide)
            w_hi[c, rows], w_lo[c, rows] = split(runs[whole[1, p]] * real[1, p])
        return carry

    lax.fori_loop(0, prods, pick, 0)
    from_core(t)
    each_side(1, leaf_hop)
    cur_1[...] = L[pl.ds(t * 4, 4)].reshape(cur_1.shape)
    tops = units(cur_1, u_hi_1, u_lo_1, peaks_1, scale_1)

    def ahead(i, carry):
        for c in (2 * i, 2 * i + 1):
            value = dot3((w_hi[c], w_lo[c]), (u_hi_1[c], u_lo_1[c]), ((1,), (0,)))
            for q in range(sums):
                total[q * wide : (q + 1) * wide] += value[q * wide : (q + 1) * wide] * scale_1[q, c]
        return carry

    lax.fori_loop(0, prods // 2, ahead, 0)
    for q in range(sums):
        F[t, q] = upper[q] / total[q * wide : (q + 1) * wide]
    for side in range(2):
        @pl.when(has_z[side])
        def _():
            flow_z(z, side).start()
    flow_y(z).start()
    leaf_turn(0, z)
    each_side(2, leaf_hop)
    for q in range(sums):
        sum_values[q] = tops[q] + jnp.log(total[q * wide : (q + 1) * wide])

    def behind(c, carry):
        f = jnp.concatenate([F[t, q] * scale_1[q, c] for q in range(sums)], axis=0)
        value = dot3((w_hi[c], w_lo[c]), split(f), ((0,), (0,)))
        value = value * (u_hi_1[c].astype(f32) + u_lo_1[c].astype(f32))
        for g in range(part.shape[0]):
            times = (child_of[c, 0] == g).astype(f32) + (child_of[c, 1] == g).astype(f32)
            part[g] += value * times
        return carry

    lax.fori_loop(0, prods, behind, 0)

    def core_copy(xx):
        return remote(
            part.at[pl.ds(2 * (xx * 2 + 1 - k), 2)], got_core.at[xx], send_core.at[xx], recv_core.at[xx], by_core
        )

    for xx in range(2):
        core_copy(xx).start()
    each_side(1, leaf_turn)
    each_side(1, flow_hop)
    from_x(z * 2 + 1 - y)
    for xx in range(2):
        core_copy(xx).wait_recv()
        mid[xx] = part[pl.ds(2 * (xx * 2 + k), 2)] + got_core[xx]
    x_copy = remote(mid.at[1 - x], got_x, send_x, recv_x, by_x)
    x_copy.start()

    from_core(z * 2 + 1 - y)
    arrived_f(z * 2 + 1 - y)
    outers(z)
    each_side(3, leaf_hop)
    each_side(2, leaf_turn)
    each_side(1, both_x)
    each_side(2, flow_hop)
    each_side(3, leaf_turn)
    each_side(2, both_x)
    at_hop(1)
    each_side(3, flow_hop)
    each_side(3, both_x)
    at_hop(2)
    at_hop(3)

    x_copy.wait_recv()
    leaf_flow[...] = mid[x] + got_x[...]

    def finish(b, carry):
        alive = (t * keep + b < count[0]).astype(f32)
        param_flow[b] = W[t * keep + b] * outer[b] * alive
        return carry

    lax.fori_loop(0, keep, finish, 0)

    for xx in range(2):
        core_copy(xx).wait_send()
    x_copy.wait_send()

    def sent(tt, carry):
        leaf_x(tt).wait_send()
        leaf_c(n, 0, tt).wait_send()
        leaf_c(nx, 1, tt).wait_send()
        return carry

    lax.fori_loop(0, 2 * depth, sent, 0)

    def sent_z(zz, carry):
        leaf_y(zz).wait_send()
        flow_y(zz).wait_send()
        @pl.when((zz >= z) & has_z[0])
        def _():
            leaf_z(zz, 0).wait_send()
            flow_z(zz, 0).wait_send()
        @pl.when((zz <= z) & has_z[1])
        def _():
            leaf_z(zz, 1).wait_send()
            flow_z(zz, 1).wait_send()
        return carry

    lax.fori_loop(0, depth, sent_z, 0)


def fused(leaves, prod_child, block_weight, block_child, block_parent, block_count, upper_flow):
    group, wide, samples = leaves.shape
    prods, sums = prod_child.shape[0], upper_flow.shape[0]
    owners, batches = lax.axis_size("nodes"), lax.axis_size("batch")
    keep = block_weight.shape[0] // batches
    whole, real = order_blocks(block_count, block_child, block_parent, sums)
    smem, vmem = pl.BlockSpec(memory_space=pltpu.SMEM), pl.BlockSpec(memory_space=pltpu.VMEM)
    dma = lambda *dims: pltpu.SemaphoreType.DMA(dims)
    vec = lambda kind, *dims: pltpu.VMEM(dims, kind)
    two = 2 * samples
    return pl.pallas_call(
        main_kernel,
        in_specs=[smem] * 6 + [vmem] * 2 + [pl.BlockSpec(memory_space=pl.ANY)],
        out_specs=[vmem] * 3,
        out_shape=[
            jax.ShapeDtypeStruct(upper_flow.shape, f32),
            jax.ShapeDtypeStruct(leaves.shape, f32),
            jax.ShapeDtypeStruct((keep, *block_weight.shape[1:]), f32),
        ],
        scratch_shapes=[
            vec(f32, batches * owners, group, wide, samples),
            vec(f32, batches, sums, wide, samples),
            vec(f32, owners * group, wide, two),
            vec(f32, sums, wide, two),
            vec(bf16, prods, wide, two),
            vec(bf16, prods, wide, two),
            vec(f32, prods, 1, two),
            vec(f32, sums, prods, 1, two),
            vec(f32, owners * group, wide, samples),
            vec(bf16, prods, wide, samples),
            vec(bf16, prods, wide, samples),
            vec(f32, prods, 1, samples),
            vec(f32, sums, prods, 1, samples),
            vec(f32, sums * wide, samples),
            vec(f32, keep, *block_weight.shape[1:]),
            vec(f32, *block_weight.shape),
            vec(f32, *block_weight.shape),
            vec(bf16, prods, sums * wide, wide),
            vec(bf16, prods, sums * wide, wide),
            vec(f32, owners * group, wide, samples),
            vec(f32, 2, group, wide, samples),
            vec(f32, 2, group, wide, samples),
            vec(f32, group, wide, samples),
            dma(batches * owners),
            dma(batches),
            dma(2 * batches),
            dma(batches // 2),
            dma(batches),
            dma(batches),
            dma(batches // 2),
            dma(batches),
            dma(2),
            dma(2),
            pltpu.SemaphoreType.DMA,
            pltpu.SemaphoreType.DMA,
            dma(8),
        ],
        compiler_params=pltpu.CompilerParams(
            collective_id=0, has_side_effects=True, vmem_limit_bytes=50 << 20
        ),
    )(
        prod_child, block_child, block_parent, block_count, whole, real,
        leaves, upper_flow, block_weight,
    )


def solution(mesh):
    placed = (
        P("nodes", None, "batch"),
        P(),
        P("nodes", None, None),
        P("nodes", None),
        P("nodes", None),
        P("nodes"),
        P("nodes", None, "batch"),
    )
    small = dict(mesh.shape) == {"nodes": 4, "batch": 8}
    return jax.shard_map(
        fused if small else body,
        mesh=mesh,
        in_specs=placed,
        out_specs=(
            P("nodes", None, "batch"),
            P("nodes", None, "batch"),
            P(("nodes", "batch"), None, None),
        ),
        check_vma=False,
    )
```

```python
import functools

import jax
import jax.numpy as jnp
from jax import lax
from jax.experimental import pallas as pl
from jax.experimental.pallas import tpu as pltpu
from jax.sharding import PartitionSpec as P

very_low = -1e30
high = lax.Precision.HIGH


def body(leaves, prod_child, block_weight, block_child, block_parent, block_count, upper_flow):
    total_prod = prod_child.shape[0]
    sum_each = upper_flow.shape[0]
    blocks = block_weight.shape[0]
    keep = blocks // lax.axis_size("batch")
    every = lax.all_gather(leaves, "nodes", axis=0, tiled=True)
    select = jax.nn.one_hot(prod_child[:, 0], every.shape[0], dtype=jnp.float32) + jax.nn.one_hot(
        prod_child[:, 1], every.shape[0], dtype=jnp.float32
    )
    products = every[prod_child[:, 0]] + every[prod_child[:, 1]]
    peak = jnp.max(products, axis=1)
    child = block_child.reshape(-1)
    parent = block_parent.reshape(-1)
    live = jnp.arange(blocks, dtype=jnp.int32) < block_count[0]
    pair = parent * total_prod + child
    pairs = sum_each * total_prod
    hot = jnp.where(live[:, None], jax.nn.one_hot(pair, pairs, dtype=jnp.float32), 0.0)
    weight = jnp.einsum(
        "bp,bij->pij", hot, block_weight, precision=high, preferred_element_type=jnp.float32
    ).reshape(sum_each, total_prod, *block_weight.shape[1:])
    has = (jnp.max(hot, axis=0) > 0.0).reshape(sum_each, total_prod)[:, :, None]
    top = jnp.max(jnp.where(has, peak[None], very_low), axis=1)
    scale = jnp.where(has, jnp.exp(jnp.where(has, peak[None] - top[:, None], 0.0)), 0.0)
    unit = jnp.exp(products - peak[:, None])
    total = jnp.einsum(
        "qcij,qcjs->qis",
        weight,
        unit[None] * scale[:, :, None],
        precision=high,
        preferred_element_type=jnp.float32,
    )
    sum_values = top[:, None, :] + jnp.log(total)
    factor = upper_flow / total
    scaled = factor[:, None] * scale[:, :, None]
    outer = jnp.einsum(
        "qcis,cjs->qcij", scaled, unit, precision=high, preferred_element_type=jnp.float32
    )
    outer = lax.psum(outer.reshape(pairs, *block_weight.shape[1:]), "batch")
    back = jnp.einsum(
        "qcij,qcis->cjs", weight, scaled, precision=high, preferred_element_type=jnp.float32
    )
    leaf_flow = lax.psum_scatter(
        jnp.einsum(
            "cg,cjs->gjs",
            select,
            unit * back,
            precision=lax.Precision.HIGHEST,
            preferred_element_type=jnp.float32,
        ),
        "nodes",
        scatter_dimension=0,
        tiled=True,
    )
    first = lax.axis_index("batch") * keep
    own = lax.dynamic_slice_in_dim(block_weight, first, keep, 0)
    own_pair = lax.dynamic_slice_in_dim(pair, first, keep, 0)
    own_live = lax.dynamic_slice_in_dim(live, first, keep, 0)
    param_flow = jnp.where(own_live[:, None, None], own * outer[own_pair], 0.0)
    return (sum_values, leaf_flow, param_flow)


MESH = pl.DeviceIdType.MESH
f32, bf16 = jnp.float32, jnp.bfloat16


def split(value):
    top_part = value.astype(bf16)
    return top_part, (value - top_part.astype(f32)).astype(bf16)


def dot3(a, b, dims):
    (a_hi, a_lo), (b_hi, b_lo) = a, b
    dot = lambda p, q: lax.dot_general(p, q, (dims, ((), ())), preferred_element_type=f32)
    return dot(a_hi, b_hi) + dot(a_hi, b_lo) + dot(a_lo, b_hi)


def order_kernel(sums, count_ref, both_ref, whole_ref, real_ref):
    blocks = both_ref.shape[1]
    shape = (blocks, blocks)
    row = lax.broadcasted_iota(jnp.int32, shape, 0)
    column = lax.broadcasted_iota(jnp.int32, shape, 1)
    row_f, column_f = row.astype(f32), column.astype(f32)
    lane = lax.broadcasted_iota(jnp.int32, (1, blocks), 1)
    key = both_ref[0:1] * sums + both_ref[1:2]
    key = jnp.where(lane < count_ref[0], key, 1 << 20).astype(f32)
    along = jnp.broadcast_to(key, shape)
    down = along.T
    before = (down < along) | ((down == along) & (row < column))
    rank = jnp.sum(before.astype(f32), axis=0, keepdims=True)
    rank_down = jnp.broadcast_to(rank, shape).T
    total = lambda take, value: jnp.sum(jnp.where(take, value, 0.0), axis=0, keepdims=True)
    here = rank_down == column_f
    order = total(here, row_f)
    same = total(here, down) == total(rank_down == column_f - 1.0, down)
    keep = jnp.where(same & (lane > 0), 1.0, 0.0)
    last = jnp.maximum(total(down <= column_f, jnp.ones(shape, f32)) - 1.0, 0.0)
    used = jnp.minimum(total(down == column_f, jnp.ones(shape, f32)), 1.0)
    whole_ref[0:1] = order.astype(jnp.int32)
    whole_ref[1:2] = last.astype(jnp.int32)
    real_ref[0:1] = keep
    real_ref[1:2] = used
    whole_ref[2:4] = both_ref[...]
    real_ref[2:3] = jnp.where(lane < count_ref[0], 1.0, 0.0)


def order_blocks(count, child, parent, sums):
    both = jnp.concatenate([child, parent], axis=0)
    smem, vmem = pl.BlockSpec(memory_space=pltpu.SMEM), pl.BlockSpec(memory_space=pltpu.VMEM)
    return pl.pallas_call(
        functools.partial(order_kernel, sums),
        in_specs=[smem, vmem],
        out_specs=[vmem, vmem],
        out_shape=[
            jax.ShapeDtypeStruct((4, child.shape[1]), jnp.int32),
            jax.ShapeDtypeStruct((3, child.shape[1]), f32),
        ],
        compiler_params=pltpu.CompilerParams(vmem_limit_bytes=50 << 20),
    )(count, both)


def main_kernel(
    child_of, whole, real, leaves, upper_in, weight,
    sum_values, leaf_flow, param_flow,
    L, F, cur, fcur, u_hi, u_lo, peaks, scale, cur_1, u_hi_1, u_lo_1, peaks_1, scale_1,
    upper, total, outer, W, runs, w_hi, w_lo, part, got_core, mid, got_x,
    recv_l, send_lx, send_lc, send_ly, send_lz, recv_f, send_fy, send_fz, send_core, recv_core, send_x, recv_x, send_lp, in_sem, w_sem,
):
    n, t = lax.axis_index("nodes"), lax.axis_index("batch")
    x, k, z, y = n // 2, n % 2, t // 2, t % 2
    depth = 4
    nx, nc, nxc = (1 - x) * 2 + k, x * 2 + 1 - k, (1 - x) * 2 + 1 - k
    by_x, by_core, by_y = (nx, t), (nc, t), (n, z * 2 + 1 - y)
    by_z = ((n, t - 2), (n, t + 2))
    has_z = (z > 0, z < depth - 1)
    pair_z = z + 1 - 2 * (z % 2)
    prods, sums = u_hi.shape[0], upper.shape[0]
    wide, samples = upper.shape[1:]
    keep = outer.shape[0]
    very = f32(very_low)

    blocks, pieces = W.shape[0], w_sem.shape[0]

    def weight_copy(i):
        at = pl.ds(i * (blocks // pieces), blocks // pieces)
        return pltpu.make_async_copy(weight.at[at], W.at[at], w_sem.at[i])

    leaf_in = pltpu.make_async_copy(leaves, L.at[t * 4 + n], in_sem.at[0])
    flow_in = pltpu.make_async_copy(upper_in, upper, in_sem.at[1])
    leaf_in.start()
    for i in range(pieces):
        weight_copy(i).start()
    flow_in.start()
    barrier = pltpu.get_barrier_semaphore()
    for partner in (by_x, by_core, by_y):
        pl.semaphore_signal(barrier, inc=1, device_id=partner, device_id_type=MESH)
    for side in range(2):
        @pl.when(has_z[side])
        def _():
            pl.semaphore_signal(barrier, inc=1, device_id=by_z[side], device_id_type=MESH)
    leaf_in.wait()
    pl.semaphore_wait(barrier, 3 + (z > 0).astype(jnp.int32) + (z < depth - 1).astype(jnp.int32))

    def remote(src, dst, send, recv, to):
        return pltpu.make_async_remote_copy(
            src_ref=src, dst_ref=dst, send_sem=send, recv_sem=recv, device_id=to, device_id_type=MESH
        )

    def leaf_to(nn, tt, send, to):
        at = L.at[tt * 4 + nn]
        return remote(at, at, send, recv_l.at[tt * 4 + nn], to)

    def leaf_x(tt):
        return leaf_to(n, tt, send_lx.at[tt], by_x)

    def leaf_c(nn, which, tt):
        return leaf_to(nn, tt, send_lc.at[which * 8 + tt], by_core)

    def leaf_y(zz):
        return leaf_to(n, zz * 2 + y, send_ly.at[zz], by_y)

    def leaf_z(zz, side):
        return leaf_to(n, zz * 2 + y, send_lz.at[side * depth + zz], by_z[side])

    def flow_to(tt, send, to):
        at = F.at[tt]
        return remote(at, at, send, recv_f.at[tt], to)

    def flow_y(zz):
        return flow_to(zz * 2 + y, send_fy.at[zz], by_y)

    def flow_z(zz, side):
        return flow_to(zz * 2 + y, send_fz.at[side * depth + zz], by_z[side])

    def arrived_l(nn, tt):
        leaf_to(nn, tt, send_lx.at[tt], by_x).wait_recv()

    def arrived_f(tt):
        flow_to(tt, send_fy.at[0], by_y).wait_recv()

    def spread(tt):
        leaf_x(tt).start()
        leaf_c(n, 0, tt).start()

    def from_x(tt):
        arrived_l(nx, tt)
        leaf_c(nx, 1, tt).start()

    def from_core(tt):
        arrived_l(nc, tt)
        arrived_l(nxc, tt)

    def each_side(step, act):
        for side, zz, exists in ((0, z - step, z - step >= 0), (1, z + step, z + step < depth)):
            @pl.when(exists)
            def _():
                act(side, zz)

    def leaf_hop(side, zz):
        arrived_l(n, zz * 2 + y)
        @pl.when(has_z[1 - side])
        def _():
            leaf_z(zz, 1 - side).start()
        @pl.when(zz != pair_z)
        def _():
            leaf_y(zz).start()
        spread(zz * 2 + y)

    def flow_hop(side, zz):
        arrived_f(zz * 2 + y)
        @pl.when(has_z[1 - side])
        def _():
            flow_z(zz, 1 - side).start()
        flow_y(zz).start()

    def leaf_turn(side, zz):
        arrived_l(n, zz * 2 + 1 - y)
        spread(zz * 2 + 1 - y)

    def leaf_pair():
        return leaf_to(n, z * 2 + 1 - y, send_lp, (n, pair_z * 2 + y))

    def both_x(side, zz):
        for yy in range(2):
            from_x(zz * 2 + yy)

    def units(cur, u_hi, u_lo, peaks, scale):
        times = cur.shape[-1] // samples

        def some(i, carry):
            for c in (2 * i, 2 * i + 1):
                prod = cur[child_of[0, c]] + cur[child_of[1, c]]
                peak = jnp.max(prod, axis=0, keepdims=True)
                peaks[c] = peak
                u_hi[c], u_lo[c] = split(jnp.exp(prod - peak))
            return carry

        lax.fori_loop(0, prods // 2, some, 0)
        tops = []
        for q in range(sums):
            used = [real[1, c * sums + q] for c in range(prods)]
            top = peaks[0] + (used[0] - 1.0) * -very
            for c in range(1, prods):
                top = jnp.maximum(top, peaks[c] + (used[c] - 1.0) * -very)
            for c in range(prods):
                scale[q, c] = jnp.exp(jnp.minimum(peaks[c] - top, 0.0)) * used[c]
            tops.append(top)
        return tops

    def outers(zz):
        for yy in range(2):
            columns = pl.ds(yy * samples, samples)
            cur[:, :, columns] = L[pl.ds((zz * 2 + yy) * 4, 4)].reshape(cur_1.shape)
            fcur[:, :, columns] = F[zz * 2 + yy]
        units(cur, u_hi, u_lo, peaks, scale)

        def some(i, carry):
            for j in range(4):
                b = 4 * i + j
                q, c = whole[3, t * keep + b], whole[2, t * keep + b]
                outer[b] += dot3(split(fcur[q] * scale[q, c]), (u_hi[c], u_lo[c]), ((1,), (1,)))
            return carry

        lax.fori_loop(0, keep // 4, some, 0)

    def at_hop(step):
        def one(side, carry):
            zz = z + step * (2 * side - 1)

            @pl.when((zz >= 0) & (zz < depth))
            def _():
                from_core(zz * 2)
                from_core(zz * 2 + 1)
                arrived_f(zz * 2 + 1 - y)
                outers(zz)
            return carry

        lax.fori_loop(0, 2, one, 0)

    spread(t)
    for side in range(2):
        @pl.when(has_z[side])
        def _():
            leaf_z(z, side).start()
    leaf_y(z).start()
    outer[...] = jnp.zeros_like(outer)
    total[...] = jnp.zeros_like(total)
    part[...] = jnp.zeros_like(part)

    for i in range(pieces):
        weight_copy(i).wait()

    def run(i, value):
        for j in range(4):
            at = 4 * i + j
            value = value * real[0, at] + W[whole[0, at]]
            runs[at] = value
        return value

    lax.fori_loop(0, blocks // 4, run, jnp.zeros(W.shape[1:], f32))
    from_x(t)
    each_side(1, leaf_hop)
    leaf_turn(0, z)
    leaf_pair().start()

    def pick(c, carry):
        for q in range(sums):
            p = c * sums + q
            rows = pl.ds(q * wide, wide)
            w_hi[c, rows], w_lo[c, rows] = split(runs[whole[1, p]] * real[1, p])
        return carry

    lax.fori_loop(0, prods, pick, 0)
    from_core(t)
    cur_1[...] = L[pl.ds(t * 4, 4)].reshape(cur_1.shape)
    tops = units(cur_1, u_hi_1, u_lo_1, peaks_1, scale_1)

    each_side(2, leaf_hop)
    flow_in.wait()

    def ahead(i, carry):
        for c in (2 * i, 2 * i + 1):
            value = dot3((w_hi[c], w_lo[c]), (u_hi_1[c], u_lo_1[c]), ((1,), (0,)))
            for q in range(sums):
                total[q * wide : (q + 1) * wide] += value[q * wide : (q + 1) * wide] * scale_1[q, c]
        return carry

    lax.fori_loop(0, prods // 2, ahead, 0)
    for q in range(sums):
        F[t, q] = upper[q] / total[q * wide : (q + 1) * wide]
    for side in range(2):
        @pl.when(has_z[side])
        def _():
            flow_z(z, side).start()
    flow_y(z).start()
    each_side(3, leaf_hop)
    for q in range(sums):
        sum_values[q] = tops[q] + jnp.log(total[q * wide : (q + 1) * wide])

    def behind(c, carry):
        f = jnp.concatenate([F[t, q] * scale_1[q, c] for q in range(sums)], axis=0)
        value = dot3((w_hi[c], w_lo[c]), split(f), ((0,), (0,)))
        value = value * (u_hi_1[c].astype(f32) + u_lo_1[c].astype(f32))
        for g in range(part.shape[0]):
            times = (child_of[0, c] == g).astype(f32) + (child_of[1, c] == g).astype(f32)
            part[g] += value * times
        return carry

    lax.fori_loop(0, prods, behind, 0)

    def core_copy(xx):
        return remote(
            part.at[pl.ds(2 * (xx * 2 + 1 - k), 2)], got_core.at[xx], send_core.at[xx], recv_core.at[xx], by_core
        )

    for xx in range(2):
        core_copy(xx).start()
    each_side(1, leaf_turn)
    each_side(1, flow_hop)
    from_x(z * 2 + 1 - y)
    for xx in range(2):
        core_copy(xx).wait_recv()
        mid[xx] = part[pl.ds(2 * (xx * 2 + k), 2)] + got_core[xx]
    x_copy = remote(mid.at[1 - x], got_x, send_x, recv_x, by_x)
    x_copy.start()

    from_core(z * 2 + 1 - y)
    arrived_f(z * 2 + 1 - y)
    outers(z)
    each_side(2, leaf_turn)
    each_side(1, both_x)
    each_side(2, flow_hop)
    each_side(3, leaf_turn)
    each_side(2, both_x)
    at_hop(1)
    each_side(3, flow_hop)
    each_side(3, both_x)
    at_hop(2)
    at_hop(3)

    x_copy.wait_recv()
    leaf_flow[...] = mid[x] + got_x[...]

    def finish(b, carry):
        param_flow[b] = W[t * keep + b] * outer[b] * real[2, t * keep + b]
        return carry

    lax.fori_loop(0, keep, finish, 0)

    for xx in range(2):
        core_copy(xx).wait_send()
    x_copy.wait_send()
    leaf_pair().wait_send()

    def sent(tt, carry):
        leaf_x(tt).wait_send()
        leaf_c(n, 0, tt).wait_send()
        leaf_c(nx, 1, tt).wait_send()
        return carry

    lax.fori_loop(0, 2 * depth, sent, 0)

    def sent_z(zz, carry):
        @pl.when(zz != pair_z)
        def _():
            leaf_y(zz).wait_send()
        flow_y(zz).wait_send()
        @pl.when((zz >= z) & has_z[0])
        def _():
            leaf_z(zz, 0).wait_send()
            flow_z(zz, 0).wait_send()
        @pl.when((zz <= z) & has_z[1])
        def _():
            leaf_z(zz, 1).wait_send()
            flow_z(zz, 1).wait_send()
        return carry

    lax.fori_loop(0, depth, sent_z, 0)


def fused(leaves, prod_child, block_weight, block_child, block_parent, block_count, upper_flow):
    group, wide, samples = leaves.shape
    prods, sums = prod_child.shape[0], upper_flow.shape[0]
    owners, batches = lax.axis_size("nodes"), lax.axis_size("batch")
    keep = block_weight.shape[0] // batches
    whole, real = order_blocks(block_count, block_child, block_parent, sums)
    smem, vmem = pl.BlockSpec(memory_space=pltpu.SMEM), pl.BlockSpec(memory_space=pltpu.VMEM)
    dma = lambda *dims: pltpu.SemaphoreType.DMA(dims)
    vec = lambda kind, *dims: pltpu.VMEM(dims, kind)
    two = 2 * samples
    return pl.pallas_call(
        main_kernel,
        in_specs=[smem] * 3 + [pl.BlockSpec(memory_space=pl.ANY)] * 3,
        out_specs=[vmem] * 3,
        out_shape=[
            jax.ShapeDtypeStruct(upper_flow.shape, f32),
            jax.ShapeDtypeStruct(leaves.shape, f32),
            jax.ShapeDtypeStruct((keep, *block_weight.shape[1:]), f32),
        ],
        scratch_shapes=[
            vec(f32, batches * owners, group, wide, samples),
            vec(f32, batches, sums, wide, samples),
            vec(f32, owners * group, wide, two),
            vec(f32, sums, wide, two),
            vec(bf16, prods, wide, two),
            vec(bf16, prods, wide, two),
            vec(f32, prods, 1, two),
            vec(f32, sums, prods, 1, two),
            vec(f32, owners * group, wide, samples),
            vec(bf16, prods, wide, samples),
            vec(bf16, prods, wide, samples),
            vec(f32, prods, 1, samples),
            vec(f32, sums, prods, 1, samples),
            vec(f32, sums, wide, samples),
            vec(f32, sums * wide, samples),
            vec(f32, keep, *block_weight.shape[1:]),
            vec(f32, *block_weight.shape),
            vec(f32, *block_weight.shape),
            vec(bf16, prods, sums * wide, wide),
            vec(bf16, prods, sums * wide, wide),
            vec(f32, owners * group, wide, samples),
            vec(f32, 2, group, wide, samples),
            vec(f32, 2, group, wide, samples),
            vec(f32, group, wide, samples),
            dma(batches * owners),
            dma(batches),
            dma(2 * batches),
            dma(batches // 2),
            dma(batches),
            dma(batches),
            dma(batches // 2),
            dma(batches),
            dma(2),
            dma(2),
            pltpu.SemaphoreType.DMA,
            pltpu.SemaphoreType.DMA,
            pltpu.SemaphoreType.DMA,
            dma(2),
            dma(8),
        ],
        compiler_params=pltpu.CompilerParams(
            collective_id=0, has_side_effects=True, vmem_limit_bytes=50 << 20
        ),
    )(
        prod_child.T, whole, real, leaves, upper_flow, block_weight,
    )


def solution(mesh):
    placed = (
        P("nodes", None, "batch"),
        P(),
        P("nodes", None, None),
        P("nodes", None),
        P("nodes", None),
        P("nodes"),
        P("nodes", None, "batch"),
    )
    small = dict(mesh.shape) == {"nodes": 4, "batch": 8}
    return jax.shard_map(
        fused if small else body,
        mesh=mesh,
        in_specs=placed,
        out_specs=(
            P("nodes", None, "batch"),
            P("nodes", None, "batch"),
            P(("nodes", "batch"), None, None),
        ),
        check_vma=False,
    )
```

```python
import functools

import jax
import jax.numpy as jnp
from jax import lax
from jax.experimental import pallas as pl
from jax.experimental.pallas import tpu as pltpu
from jax.sharding import PartitionSpec as P

very_low = -1e30
high = lax.Precision.HIGH


def body(leaves, prod_child, block_weight, block_child, block_parent, block_count, upper_flow):
    total_prod = prod_child.shape[0]
    sum_each = upper_flow.shape[0]
    blocks = block_weight.shape[0]
    keep = blocks // lax.axis_size("batch")
    every = lax.all_gather(leaves, "nodes", axis=0, tiled=True)
    select = jax.nn.one_hot(prod_child[:, 0], every.shape[0], dtype=jnp.float32) + jax.nn.one_hot(
        prod_child[:, 1], every.shape[0], dtype=jnp.float32
    )
    products = every[prod_child[:, 0]] + every[prod_child[:, 1]]
    peak = jnp.max(products, axis=1)
    child = block_child.reshape(-1)
    parent = block_parent.reshape(-1)
    live = jnp.arange(blocks, dtype=jnp.int32) < block_count[0]
    pair = parent * total_prod + child
    pairs = sum_each * total_prod
    hot = jnp.where(live[:, None], jax.nn.one_hot(pair, pairs, dtype=jnp.float32), 0.0)
    weight = jnp.einsum(
        "bp,bij->pij", hot, block_weight, precision=high, preferred_element_type=jnp.float32
    ).reshape(sum_each, total_prod, *block_weight.shape[1:])
    has = (jnp.max(hot, axis=0) > 0.0).reshape(sum_each, total_prod)[:, :, None]
    top = jnp.max(jnp.where(has, peak[None], very_low), axis=1)
    scale = jnp.where(has, jnp.exp(jnp.where(has, peak[None] - top[:, None], 0.0)), 0.0)
    unit = jnp.exp(products - peak[:, None])
    total = jnp.einsum(
        "qcij,qcjs->qis",
        weight,
        unit[None] * scale[:, :, None],
        precision=high,
        preferred_element_type=jnp.float32,
    )
    sum_values = top[:, None, :] + jnp.log(total)
    factor = upper_flow / total
    scaled = factor[:, None] * scale[:, :, None]
    outer = jnp.einsum(
        "qcis,cjs->qcij", scaled, unit, precision=high, preferred_element_type=jnp.float32
    )
    outer = lax.psum(outer.reshape(pairs, *block_weight.shape[1:]), "batch")
    back = jnp.einsum(
        "qcij,qcis->cjs", weight, scaled, precision=high, preferred_element_type=jnp.float32
    )
    leaf_flow = lax.psum_scatter(
        jnp.einsum(
            "cg,cjs->gjs",
            select,
            unit * back,
            precision=lax.Precision.HIGHEST,
            preferred_element_type=jnp.float32,
        ),
        "nodes",
        scatter_dimension=0,
        tiled=True,
    )
    first = lax.axis_index("batch") * keep
    own = lax.dynamic_slice_in_dim(block_weight, first, keep, 0)
    own_pair = lax.dynamic_slice_in_dim(pair, first, keep, 0)
    own_live = lax.dynamic_slice_in_dim(live, first, keep, 0)
    param_flow = jnp.where(own_live[:, None, None], own * outer[own_pair], 0.0)
    return (sum_values, leaf_flow, param_flow)


MESH = pl.DeviceIdType.MESH
f32, bf16 = jnp.float32, jnp.bfloat16


def split(value):
    top_part = value.astype(bf16)
    return top_part, (value - top_part.astype(f32)).astype(bf16)


def dot3(a, b, dims):
    (a_hi, a_lo), (b_hi, b_lo) = a, b
    dot = lambda p, q: lax.dot_general(p, q, (dims, ((), ())), preferred_element_type=f32)
    return dot(a_hi, b_hi) + dot(a_hi, b_lo) + dot(a_lo, b_hi)


def order_kernel(sums, count_ref, both_ref, whole_ref, real_ref):
    blocks = both_ref.shape[1]
    shape = (blocks, blocks)
    row = lax.broadcasted_iota(jnp.int32, shape, 0)
    column = lax.broadcasted_iota(jnp.int32, shape, 1)
    row_f, column_f = row.astype(f32), column.astype(f32)
    lane = lax.broadcasted_iota(jnp.int32, (1, blocks), 1)
    key = both_ref[0:1] * sums + both_ref[1:2]
    key = jnp.where(lane < count_ref[0], key, 1 << 20).astype(f32)
    along = jnp.broadcast_to(key, shape)
    down = along.T
    before = (down < along) | ((down == along) & (row < column))
    rank = jnp.sum(before.astype(f32), axis=0, keepdims=True)
    rank_down = jnp.broadcast_to(rank, shape).T
    total = lambda take, value: jnp.sum(jnp.where(take, value, 0.0), axis=0, keepdims=True)
    here = rank_down == column_f
    order = total(here, row_f)
    same = total(here, down) == total(rank_down == column_f - 1.0, down)
    keep = jnp.where(same & (lane > 0), 1.0, 0.0)
    last = jnp.maximum(total(down <= column_f, jnp.ones(shape, f32)) - 1.0, 0.0)
    used = jnp.minimum(total(down == column_f, jnp.ones(shape, f32)), 1.0)
    whole_ref[0:1] = order.astype(jnp.int32)
    whole_ref[1:2] = last.astype(jnp.int32)
    real_ref[0:1] = keep
    real_ref[1:2] = used
    whole_ref[2:4] = both_ref[...]
    real_ref[2:3] = jnp.where(lane < count_ref[0], 1.0, 0.0)


def order_blocks(count, child, parent, sums):
    both = jnp.concatenate([child, parent], axis=0)
    smem, vmem = pl.BlockSpec(memory_space=pltpu.SMEM), pl.BlockSpec(memory_space=pltpu.VMEM)
    return pl.pallas_call(
        functools.partial(order_kernel, sums),
        in_specs=[smem, vmem],
        out_specs=[vmem, vmem],
        out_shape=[
            jax.ShapeDtypeStruct((4, child.shape[1]), jnp.int32),
            jax.ShapeDtypeStruct((3, child.shape[1]), f32),
        ],
        compiler_params=pltpu.CompilerParams(vmem_limit_bytes=50 << 20),
    )(count, both)


def main_kernel(
    child_of, whole, real, leaves, upper_in, weight,
    sum_values, leaf_flow, param_flow,
    L, F, cur, fcur, u_hi, u_lo, peaks, scale, cur_1, u_hi_1, u_lo_1, peaks_1, scale_1,
    upper, total, outer, W, runs, w_hi, w_lo, part, got_core, mid, got_x,
    recv_l, send_lx, send_lc, send_ly, send_lz, recv_f, send_fy, send_fz, send_core, recv_core, send_x, recv_x, send_lp, in_sem, w_sem,
):
    n, t = lax.axis_index("nodes"), lax.axis_index("batch")
    x, k, z, y = n // 2, n % 2, t // 2, t % 2
    depth = 4
    nx, nc, nxc = (1 - x) * 2 + k, x * 2 + 1 - k, (1 - x) * 2 + 1 - k
    by_x, by_core, by_y = (nx, t), (nc, t), (n, z * 2 + 1 - y)
    by_z = ((n, t - 2), (n, t + 2))
    has_z = (z > 0, z < depth - 1)
    pair_z = z + 1 - 2 * (z % 2)
    prods, sums = u_hi.shape[0], upper.shape[0]
    each = sums // 2
    wide, samples = upper.shape[1:]
    keep = outer.shape[0]
    very = f32(very_low)

    blocks, pieces = W.shape[0], w_sem.shape[0]

    def weight_copy(i):
        at = pl.ds(i * (blocks // pieces), blocks // pieces)
        return pltpu.make_async_copy(weight.at[at], W.at[at], w_sem.at[i])

    leaf_in = pltpu.make_async_copy(leaves, L.at[t * 4 + n], in_sem.at[0])
    flow_in = pltpu.make_async_copy(upper_in, upper, in_sem.at[1])
    leaf_in.start()
    for i in range(pieces):
        weight_copy(i).start()
    flow_in.start()
    barrier = pltpu.get_barrier_semaphore()
    for partner in (by_x, by_core, by_y):
        pl.semaphore_signal(barrier, inc=1, device_id=partner, device_id_type=MESH)
    for side in range(2):
        @pl.when(has_z[side])
        def _():
            pl.semaphore_signal(barrier, inc=1, device_id=by_z[side], device_id_type=MESH)
    leaf_in.wait()
    pl.semaphore_wait(barrier, 3 + (z > 0).astype(jnp.int32) + (z < depth - 1).astype(jnp.int32))

    def remote(src, dst, send, recv, to):
        return pltpu.make_async_remote_copy(
            src_ref=src, dst_ref=dst, send_sem=send, recv_sem=recv, device_id=to, device_id_type=MESH
        )

    def leaf_to(nn, tt, send, to):
        at = L.at[tt * 4 + nn]
        return remote(at, at, send, recv_l.at[tt * 4 + nn], to)

    def leaf_x(tt):
        return leaf_to(n, tt, send_lx.at[tt], by_x)

    def leaf_c(nn, which, tt):
        return leaf_to(nn, tt, send_lc.at[which * 8 + tt], by_core)

    def leaf_y(zz):
        return leaf_to(n, zz * 2 + y, send_ly.at[zz], by_y)

    def leaf_z(zz, side):
        return leaf_to(n, zz * 2 + y, send_lz.at[side * depth + zz], by_z[side])

    def flow_to(tt, half, send, to):
        at = F.at[tt * 2 + half]
        return remote(at, at, send, recv_f.at[tt * 2 + half], to)

    def flow_y(zz, half):
        return flow_to(zz * 2 + y, half, send_fy.at[zz * 2 + half], by_y)

    def flow_z(zz, side, half):
        return flow_to(zz * 2 + y, half, send_fz.at[(side * depth + zz) * 2 + half], by_z[side])

    def arrived_l(nn, tt):
        leaf_to(nn, tt, send_lx.at[tt], by_x).wait_recv()

    def arrived_f(tt, half):
        flow_to(tt, half, send_fy.at[0], by_y).wait_recv()

    def spread(tt):
        leaf_x(tt).start()
        leaf_c(n, 0, tt).start()

    def from_x(tt):
        arrived_l(nx, tt)
        leaf_c(nx, 1, tt).start()

    def from_core(tt):
        arrived_l(nc, tt)
        arrived_l(nxc, tt)

    def each_side(step, act):
        for side, zz, exists in ((0, z - step, z - step >= 0), (1, z + step, z + step < depth)):
            @pl.when(exists)
            def _():
                act(side, zz)

    def leaf_hop(side, zz):
        arrived_l(n, zz * 2 + y)
        @pl.when(has_z[1 - side])
        def _():
            leaf_z(zz, 1 - side).start()
        @pl.when(zz != pair_z)
        def _():
            leaf_y(zz).start()
        spread(zz * 2 + y)

    def flow_hop(step):
        for half in range(2):
            def act(side, zz):
                arrived_f(zz * 2 + y, half)
                @pl.when(has_z[1 - side])
                def _():
                    flow_z(zz, 1 - side, half).start()
                flow_y(zz, half).start()

            each_side(step, act)

    def leaf_turn(side, zz):
        arrived_l(n, zz * 2 + 1 - y)
        spread(zz * 2 + 1 - y)

    def leaf_pair():
        return leaf_to(n, z * 2 + 1 - y, send_lp, (n, pair_z * 2 + y))

    def both_x(side, zz):
        for yy in range(2):
            from_x(zz * 2 + yy)

    def units(cur, u_hi, u_lo, peaks, scale):
        times = cur.shape[-1] // samples

        def some(i, carry):
            for c in (2 * i, 2 * i + 1):
                prod = cur[child_of[0, c]] + cur[child_of[1, c]]
                peak = jnp.max(prod, axis=0, keepdims=True)
                peaks[c] = peak
                u_hi[c], u_lo[c] = split(jnp.exp(prod - peak))
            return carry

        lax.fori_loop(0, prods // 2, some, 0)
        tops = []
        for q in range(sums):
            used = [real[1, c * sums + q] for c in range(prods)]
            top = peaks[0] + (used[0] - 1.0) * -very
            for c in range(1, prods):
                top = jnp.maximum(top, peaks[c] + (used[c] - 1.0) * -very)
            for c in range(prods):
                scale[q, c] = jnp.exp(jnp.minimum(peaks[c] - top, 0.0)) * used[c]
            tops.append(top)
        return tops

    def outers(zz):
        for yy in range(2):
            columns = pl.ds(yy * samples, samples)
            cur[:, :, columns] = L[pl.ds((zz * 2 + yy) * 4, 4)].reshape(cur_1.shape)
            fcur[:, :, columns] = F[pl.ds((zz * 2 + yy) * 2, 2)].reshape(upper.shape)
        units(cur, u_hi, u_lo, peaks, scale)

        def some(i, carry):
            for j in range(4):
                b = 4 * i + j
                q, c = whole[3, t * keep + b], whole[2, t * keep + b]
                outer[b] += dot3(split(fcur[q] * scale[q, c]), (u_hi[c], u_lo[c]), ((1,), (1,)))
            return carry

        lax.fori_loop(0, keep // 4, some, 0)

    def at_hop(step):
        def one(side, carry):
            zz = z + step * (2 * side - 1)

            @pl.when((zz >= 0) & (zz < depth))
            def _():
                from_core(zz * 2)
                from_core(zz * 2 + 1)
                for half in range(2):
                    arrived_f(zz * 2 + 1 - y, half)
                outers(zz)
            return carry

        lax.fori_loop(0, 2, one, 0)

    spread(t)
    for side in range(2):
        @pl.when(has_z[side])
        def _():
            leaf_z(z, side).start()
    leaf_y(z).start()
    outer[...] = jnp.zeros_like(outer)
    total[...] = jnp.zeros_like(total)
    part[...] = jnp.zeros_like(part)

    for i in range(pieces):
        weight_copy(i).wait()

    def run(i, value):
        for j in range(4):
            at = 4 * i + j
            value = value * real[0, at] + W[whole[0, at]]
            runs[at] = value
        return value

    lax.fori_loop(0, blocks // 4, run, jnp.zeros(W.shape[1:], f32))
    from_x(t)
    each_side(1, leaf_hop)
    leaf_turn(0, z)
    leaf_pair().start()

    def pick(c, carry):
        for q in range(sums):
            p = c * sums + q
            rows = pl.ds(q * wide, wide)
            w_hi[c, rows], w_lo[c, rows] = split(runs[whole[1, p]] * real[1, p])
        return carry

    lax.fori_loop(0, prods, pick, 0)
    from_core(t)
    cur_1[...] = L[pl.ds(t * 4, 4)].reshape(cur_1.shape)
    tops = units(cur_1, u_hi_1, u_lo_1, peaks_1, scale_1)

    each_side(2, leaf_hop)
    flow_in.wait()

    def ahead(i, carry):
        for c in (2 * i, 2 * i + 1):
            value = dot3((w_hi[c], w_lo[c]), (u_hi_1[c], u_lo_1[c]), ((1,), (0,)))
            for q in range(sums):
                total[q * wide : (q + 1) * wide] += value[q * wide : (q + 1) * wide] * scale_1[q, c]
        return carry

    lax.fori_loop(0, prods // 2, ahead, 0)
    for q in range(sums):
        F[2 * t + q // each, q % each] = upper[q] / total[q * wide : (q + 1) * wide]
    for half in range(2):
        for side in range(2):
            @pl.when(has_z[side])
            def _():
                flow_z(z, side, half).start()
        flow_y(z, half).start()
    each_side(3, leaf_hop)
    for q in range(sums):
        sum_values[q] = tops[q] + jnp.log(total[q * wide : (q + 1) * wide])

    def behind(c, carry):
        f = jnp.concatenate([F[2 * t + q // each, q % each] * scale_1[q, c] for q in range(sums)], axis=0)
        value = dot3((w_hi[c], w_lo[c]), split(f), ((0,), (0,)))
        value = value * (u_hi_1[c].astype(f32) + u_lo_1[c].astype(f32))
        for g in range(part.shape[0]):
            times = (child_of[0, c] == g).astype(f32) + (child_of[1, c] == g).astype(f32)
            part[g] += value * times
        return carry

    lax.fori_loop(0, prods, behind, 0)

    def core_copy(xx):
        return remote(
            part.at[pl.ds(2 * (xx * 2 + 1 - k), 2)], got_core.at[xx], send_core.at[xx], recv_core.at[xx], by_core
        )

    for xx in range(2):
        core_copy(xx).start()
    each_side(1, leaf_turn)
    flow_hop(1)
    from_x(z * 2 + 1 - y)
    for xx in range(2):
        core_copy(xx).wait_recv()
        mid[xx] = part[pl.ds(2 * (xx * 2 + k), 2)] + got_core[xx]
    x_copy = remote(mid.at[1 - x], got_x, send_x, recv_x, by_x)
    x_copy.start()

    from_core(z * 2 + 1 - y)
    each_side(2, leaf_turn)
    each_side(1, both_x)
    flow_hop(2)
    for half in range(2):
        arrived_f(z * 2 + 1 - y, half)
    outers(z)
    each_side(3, leaf_turn)
    each_side(2, both_x)
    flow_hop(3)
    each_side(3, both_x)
    at_hop(1)
    at_hop(2)
    at_hop(3)

    x_copy.wait_recv()
    leaf_flow[...] = mid[x] + got_x[...]

    def finish(b, carry):
        param_flow[b] = W[t * keep + b] * outer[b] * real[2, t * keep + b]
        return carry

    lax.fori_loop(0, keep, finish, 0)

    for xx in range(2):
        core_copy(xx).wait_send()
    x_copy.wait_send()
    leaf_pair().wait_send()

    def sent(tt, carry):
        leaf_x(tt).wait_send()
        leaf_c(n, 0, tt).wait_send()
        leaf_c(nx, 1, tt).wait_send()
        return carry

    lax.fori_loop(0, 2 * depth, sent, 0)

    def sent_z(zz, carry):
        @pl.when(zz != pair_z)
        def _():
            leaf_y(zz).wait_send()
        for half in range(2):
            flow_y(zz, half).wait_send()
        @pl.when((zz >= z) & has_z[0])
        def _():
            leaf_z(zz, 0).wait_send()
            for half in range(2):
                flow_z(zz, 0, half).wait_send()
        @pl.when((zz <= z) & has_z[1])
        def _():
            leaf_z(zz, 1).wait_send()
            for half in range(2):
                flow_z(zz, 1, half).wait_send()
        return carry

    lax.fori_loop(0, depth, sent_z, 0)


def fused(leaves, prod_child, block_weight, block_child, block_parent, block_count, upper_flow):
    group, wide, samples = leaves.shape
    prods, sums = prod_child.shape[0], upper_flow.shape[0]
    owners, batches = lax.axis_size("nodes"), lax.axis_size("batch")
    keep = block_weight.shape[0] // batches
    whole, real = order_blocks(block_count, block_child, block_parent, sums)
    smem, vmem = pl.BlockSpec(memory_space=pltpu.SMEM), pl.BlockSpec(memory_space=pltpu.VMEM)
    dma = lambda *dims: pltpu.SemaphoreType.DMA(dims)
    vec = lambda kind, *dims: pltpu.VMEM(dims, kind)
    two = 2 * samples
    return pl.pallas_call(
        main_kernel,
        in_specs=[smem] * 3 + [pl.BlockSpec(memory_space=pl.ANY)] * 3,
        out_specs=[vmem] * 3,
        out_shape=[
            jax.ShapeDtypeStruct(upper_flow.shape, f32),
            jax.ShapeDtypeStruct(leaves.shape, f32),
            jax.ShapeDtypeStruct((keep, *block_weight.shape[1:]), f32),
        ],
        scratch_shapes=[
            vec(f32, batches * owners, group, wide, samples),
            vec(f32, batches * 2, sums // 2, wide, samples),
            vec(f32, owners * group, wide, two),
            vec(f32, sums, wide, two),
            vec(bf16, prods, wide, two),
            vec(bf16, prods, wide, two),
            vec(f32, prods, 1, two),
            vec(f32, sums, prods, 1, two),
            vec(f32, owners * group, wide, samples),
            vec(bf16, prods, wide, samples),
            vec(bf16, prods, wide, samples),
            vec(f32, prods, 1, samples),
            vec(f32, sums, prods, 1, samples),
            vec(f32, sums, wide, samples),
            vec(f32, sums * wide, samples),
            vec(f32, keep, *block_weight.shape[1:]),
            vec(f32, *block_weight.shape),
            vec(f32, *block_weight.shape),
            vec(bf16, prods, sums * wide, wide),
            vec(bf16, prods, sums * wide, wide),
            vec(f32, owners * group, wide, samples),
            vec(f32, 2, group, wide, samples),
            vec(f32, 2, group, wide, samples),
            vec(f32, group, wide, samples),
            dma(batches * owners),
            dma(batches),
            dma(2 * batches),
            dma(batches // 2),
            dma(batches),
            dma(2 * batches),
            dma(batches),
            dma(2 * batches),
            dma(2),
            dma(2),
            pltpu.SemaphoreType.DMA,
            pltpu.SemaphoreType.DMA,
            pltpu.SemaphoreType.DMA,
            dma(2),
            dma(8),
        ],
        compiler_params=pltpu.CompilerParams(
            collective_id=0, has_side_effects=True, vmem_limit_bytes=50 << 20
        ),
    )(
        prod_child.T, whole, real, leaves, upper_flow, block_weight,
    )


def solution(mesh):
    placed = (
        P("nodes", None, "batch"),
        P(),
        P("nodes", None, None),
        P("nodes", None),
        P("nodes", None),
        P("nodes"),
        P("nodes", None, "batch"),
    )
    small = dict(mesh.shape) == {"nodes": 4, "batch": 8}
    return jax.shard_map(
        fused if small else body,
        mesh=mesh,
        in_specs=placed,
        out_specs=(
            P("nodes", None, "batch"),
            P("nodes", None, "batch"),
            P(("nodes", "batch"), None, None),
        ),
        check_vma=False,
    )
```

```python
import functools

import jax
import jax.numpy as jnp
from jax import lax
from jax.experimental import pallas as pl
from jax.experimental.pallas import tpu as pltpu
from jax.sharding import PartitionSpec as P

very_low = -1e30
high = lax.Precision.HIGH


def body(leaves, prod_child, block_weight, block_child, block_parent, block_count, upper_flow):
    total_prod = prod_child.shape[0]
    sum_each = upper_flow.shape[0]
    blocks = block_weight.shape[0]
    keep = blocks // lax.axis_size("batch")
    every = lax.all_gather(leaves, "nodes", axis=0, tiled=True)
    select = jax.nn.one_hot(prod_child[:, 0], every.shape[0], dtype=jnp.float32) + jax.nn.one_hot(
        prod_child[:, 1], every.shape[0], dtype=jnp.float32
    )
    products = every[prod_child[:, 0]] + every[prod_child[:, 1]]
    peak = jnp.max(products, axis=1)
    child = block_child.reshape(-1)
    parent = block_parent.reshape(-1)
    live = jnp.arange(blocks, dtype=jnp.int32) < block_count[0]
    pair = parent * total_prod + child
    pairs = sum_each * total_prod
    hot = jnp.where(live[:, None], jax.nn.one_hot(pair, pairs, dtype=jnp.float32), 0.0)
    weight = jnp.einsum(
        "bp,bij->pij", hot, block_weight, precision=high, preferred_element_type=jnp.float32
    ).reshape(sum_each, total_prod, *block_weight.shape[1:])
    has = (jnp.max(hot, axis=0) > 0.0).reshape(sum_each, total_prod)[:, :, None]
    top = jnp.max(jnp.where(has, peak[None], very_low), axis=1)
    scale = jnp.where(has, jnp.exp(jnp.where(has, peak[None] - top[:, None], 0.0)), 0.0)
    unit = jnp.exp(products - peak[:, None])
    total = jnp.einsum(
        "qcij,qcjs->qis",
        weight,
        unit[None] * scale[:, :, None],
        precision=high,
        preferred_element_type=jnp.float32,
    )
    sum_values = top[:, None, :] + jnp.log(total)
    factor = upper_flow / total
    scaled = factor[:, None] * scale[:, :, None]
    outer = jnp.einsum(
        "qcis,cjs->qcij", scaled, unit, precision=high, preferred_element_type=jnp.float32
    )
    outer = lax.psum(outer.reshape(pairs, *block_weight.shape[1:]), "batch")
    back = jnp.einsum(
        "qcij,qcis->cjs", weight, scaled, precision=high, preferred_element_type=jnp.float32
    )
    leaf_flow = lax.psum_scatter(
        jnp.einsum(
            "cg,cjs->gjs",
            select,
            unit * back,
            precision=lax.Precision.HIGHEST,
            preferred_element_type=jnp.float32,
        ),
        "nodes",
        scatter_dimension=0,
        tiled=True,
    )
    first = lax.axis_index("batch") * keep
    own = lax.dynamic_slice_in_dim(block_weight, first, keep, 0)
    own_pair = lax.dynamic_slice_in_dim(pair, first, keep, 0)
    own_live = lax.dynamic_slice_in_dim(live, first, keep, 0)
    param_flow = jnp.where(own_live[:, None, None], own * outer[own_pair], 0.0)
    return (sum_values, leaf_flow, param_flow)


MESH = pl.DeviceIdType.MESH
f32, bf16 = jnp.float32, jnp.bfloat16


def split(value):
    top_part = value.astype(bf16)
    return top_part, (value - top_part.astype(f32)).astype(bf16)


def dot3(a, b, dims):
    (a_hi, a_lo), (b_hi, b_lo) = a, b
    dot = lambda p, q: lax.dot_general(p, q, (dims, ((), ())), preferred_element_type=f32)
    return dot(a_hi, b_hi) + dot(a_hi, b_lo) + dot(a_lo, b_hi)


def order_kernel(sums, count_ref, both_ref, whole_ref, real_ref):
    blocks = both_ref.shape[1]
    shape = (blocks, blocks)
    row = lax.broadcasted_iota(jnp.int32, shape, 0)
    column = lax.broadcasted_iota(jnp.int32, shape, 1)
    row_f, column_f = row.astype(f32), column.astype(f32)
    lane = lax.broadcasted_iota(jnp.int32, (1, blocks), 1)
    key = both_ref[0:1] * sums + both_ref[1:2]
    key = jnp.where(lane < count_ref[0], key, 1 << 20).astype(f32)
    along = jnp.broadcast_to(key, shape)
    down = along.T
    before = (down < along) | ((down == along) & (row < column))
    rank = jnp.sum(before.astype(f32), axis=0, keepdims=True)
    rank_down = jnp.broadcast_to(rank, shape).T
    total = lambda take, value: jnp.sum(jnp.where(take, value, 0.0), axis=0, keepdims=True)
    here = rank_down == column_f
    order = total(here, row_f)
    same = total(here, down) == total(rank_down == column_f - 1.0, down)
    keep = jnp.where(same & (lane > 0), 1.0, 0.0)
    last = jnp.maximum(total(down <= column_f, jnp.ones(shape, f32)) - 1.0, 0.0)
    used = jnp.minimum(total(down == column_f, jnp.ones(shape, f32)), 1.0)
    whole_ref[0:1] = order.astype(jnp.int32)
    whole_ref[1:2] = last.astype(jnp.int32)
    real_ref[0:1] = keep
    real_ref[1:2] = used
    whole_ref[2:4] = both_ref[...]
    real_ref[2:3] = jnp.where(lane < count_ref[0], 1.0, 0.0)


def order_blocks(count, child, parent, sums):
    both = jnp.concatenate([child, parent], axis=0)
    smem, vmem = pl.BlockSpec(memory_space=pltpu.SMEM), pl.BlockSpec(memory_space=pltpu.VMEM)
    return pl.pallas_call(
        functools.partial(order_kernel, sums),
        in_specs=[smem, vmem],
        out_specs=[vmem, vmem],
        out_shape=[
            jax.ShapeDtypeStruct((4, child.shape[1]), jnp.int32),
            jax.ShapeDtypeStruct((3, child.shape[1]), f32),
        ],
        compiler_params=pltpu.CompilerParams(vmem_limit_bytes=50 << 20),
    )(count, both)


def main_kernel(
    child_of, whole, real, leaves, upper_in, weight,
    sum_values, leaf_flow, param_flow,
    L, F, cur, fcur, u_hi, u_lo, peaks, scale, cur_1, u_hi_1, u_lo_1, peaks_1, scale_1,
    upper, total, outer, W, runs, w_hi, w_lo, part, got_core, mid, got_x,
    recv_l, send_lx, send_lc, send_ly, send_lz, recv_f, send_fy, send_fz, send_core, recv_core, send_x, recv_x, send_lp, in_sem, w_sem,
):
    n, t = lax.axis_index("nodes"), lax.axis_index("batch")
    x, k, z, y = n // 2, n % 2, t // 2, t % 2
    depth = 4
    nx, nc, nxc = (1 - x) * 2 + k, x * 2 + 1 - k, (1 - x) * 2 + 1 - k
    by_x, by_core, by_y = (nx, t), (nc, t), (n, z * 2 + 1 - y)
    by_z = ((n, t - 2), (n, t + 2))
    has_z = (z > 0, z < depth - 1)
    pair_z = z + 1 - 2 * (z % 2)
    at_end = (z == 0) | (z == depth - 1)
    prods, sums = u_hi.shape[0], upper.shape[0]
    each = sums // 2
    wide, samples = upper.shape[1:]
    keep = outer.shape[0]
    very = f32(very_low)

    blocks, pieces = W.shape[0], w_sem.shape[0]

    def weight_copy(i):
        at = pl.ds(i * (blocks // pieces), blocks // pieces)
        return pltpu.make_async_copy(weight.at[at], W.at[at], w_sem.at[i])

    leaf_in = pltpu.make_async_copy(leaves, L.at[t * 4 + n], in_sem.at[0])
    flow_in = pltpu.make_async_copy(upper_in, upper, in_sem.at[1])
    leaf_in.start()
    for i in range(pieces):
        weight_copy(i).start()
    flow_in.start()
    barrier = pltpu.get_barrier_semaphore()
    for partner in (by_x, by_core, by_y):
        pl.semaphore_signal(barrier, inc=1, device_id=partner, device_id_type=MESH)
    for side in range(2):
        @pl.when(has_z[side])
        def _():
            pl.semaphore_signal(barrier, inc=1, device_id=by_z[side], device_id_type=MESH)
    leaf_in.wait()
    pl.semaphore_wait(barrier, 3 + (z > 0).astype(jnp.int32) + (z < depth - 1).astype(jnp.int32))

    def remote(src, dst, send, recv, to):
        return pltpu.make_async_remote_copy(
            src_ref=src, dst_ref=dst, send_sem=send, recv_sem=recv, device_id=to, device_id_type=MESH
        )

    def leaf_to(nn, tt, send, to):
        at = L.at[tt * 4 + nn]
        return remote(at, at, send, recv_l.at[tt * 4 + nn], to)

    def leaf_x(tt):
        return leaf_to(n, tt, send_lx.at[tt], by_x)

    def leaf_c(nn, which, tt):
        return leaf_to(nn, tt, send_lc.at[which * 8 + tt], by_core)

    def leaf_y(zz):
        return leaf_to(n, zz * 2 + y, send_ly.at[zz], by_y)

    def leaf_z(zz, side):
        return leaf_to(n, zz * 2 + y, send_lz.at[side * depth + zz], by_z[side])

    def flow_to(tt, half, send, to):
        at = F.at[tt * 2 + half]
        return remote(at, at, send, recv_f.at[tt * 2 + half], to)

    def flow_y(zz, half):
        return flow_to(zz * 2 + y, half, send_fy.at[zz * 2 + half], by_y)

    def flow_z(zz, side, half):
        return flow_to(zz * 2 + y, half, send_fz.at[(side * depth + zz) * 2 + half], by_z[side])

    def arrived_l(nn, tt):
        leaf_to(nn, tt, send_lx.at[tt], by_x).wait_recv()

    def arrived_f(tt, half):
        flow_to(tt, half, send_fy.at[0], by_y).wait_recv()

    def spread(tt):
        leaf_x(tt).start()
        leaf_c(n, 0, tt).start()

    def from_x(tt):
        arrived_l(nx, tt)
        leaf_c(nx, 1, tt).start()

    def from_core(tt):
        arrived_l(nc, tt)
        arrived_l(nxc, tt)

    def each_side(step, act):
        for side, zz, exists in ((0, z - step, z - step >= 0), (1, z + step, z + step < depth)):
            @pl.when(exists)
            def _():
                act(side, zz)

    def leaf_hop(side, zz):
        arrived_l(n, zz * 2 + y)
        @pl.when(has_z[1 - side])
        def _():
            leaf_z(zz, 1 - side).start()
        @pl.when((zz != pair_z) | at_end)
        def _():
            leaf_y(zz).start()
        spread(zz * 2 + y)

    def flow_hop(step):
        for half in range(2):
            def act(side, zz):
                arrived_f(zz * 2 + y, half)
                @pl.when(has_z[1 - side])
                def _():
                    flow_z(zz, 1 - side, half).start()
                flow_y(zz, half).start()

            each_side(step, act)

    def leaf_turn(side, zz):
        arrived_l(n, zz * 2 + 1 - y)
        spread(zz * 2 + 1 - y)

    def leaf_pair():
        return leaf_to(n, z * 2 + 1 - y, send_lp, (n, pair_z * 2 + y))

    def both_x(side, zz):
        for yy in range(2):
            from_x(zz * 2 + yy)

    def units(cur, u_hi, u_lo, peaks, scale):
        times = cur.shape[-1] // samples

        def some(i, carry):
            for c in (2 * i, 2 * i + 1):
                prod = cur[child_of[0, c]] + cur[child_of[1, c]]
                peak = jnp.max(prod, axis=0, keepdims=True)
                peaks[c] = peak
                u_hi[c], u_lo[c] = split(jnp.exp(prod - peak))
            return carry

        lax.fori_loop(0, prods // 2, some, 0)
        tops = []
        for q in range(sums):
            used = [real[1, c * sums + q] for c in range(prods)]
            top = peaks[0] + (used[0] - 1.0) * -very
            for c in range(1, prods):
                top = jnp.maximum(top, peaks[c] + (used[c] - 1.0) * -very)
            for c in range(prods):
                scale[q, c] = jnp.exp(jnp.minimum(peaks[c] - top, 0.0)) * used[c]
            tops.append(top)
        return tops

    def outers(zz):
        for yy in range(2):
            columns = pl.ds(yy * samples, samples)
            cur[:, :, columns] = L[pl.ds((zz * 2 + yy) * 4, 4)].reshape(cur_1.shape)
            fcur[:, :, columns] = F[pl.ds((zz * 2 + yy) * 2, 2)].reshape(upper.shape)
        units(cur, u_hi, u_lo, peaks, scale)

        def some(i, carry):
            for j in range(4):
                b = 4 * i + j
                q, c = whole[3, t * keep + b], whole[2, t * keep + b]
                outer[b] += dot3(split(fcur[q] * scale[q, c]), (u_hi[c], u_lo[c]), ((1,), (1,)))
            return carry

        lax.fori_loop(0, keep // 4, some, 0)

    def at_hop(step):
        def one(side, carry):
            zz = z + step * (2 * side - 1)

            @pl.when((zz >= 0) & (zz < depth))
            def _():
                from_core(zz * 2)
                from_core(zz * 2 + 1)
                for half in range(2):
                    arrived_f(zz * 2 + 1 - y, half)
                outers(zz)
            return carry

        lax.fori_loop(0, 2, one, 0)

    spread(t)
    for side in range(2):
        @pl.when(has_z[side])
        def _():
            leaf_z(z, side).start()
    leaf_y(z).start()
    outer[...] = jnp.zeros_like(outer)
    total[...] = jnp.zeros_like(total)
    part[...] = jnp.zeros_like(part)

    for i in range(pieces):
        weight_copy(i).wait()

    def run(i, value):
        for j in range(4):
            at = 4 * i + j
            value = value * real[0, at] + W[whole[0, at]]
            runs[at] = value
        return value

    lax.fori_loop(0, blocks // 4, run, jnp.zeros(W.shape[1:], f32))
    from_x(t)
    each_side(1, leaf_hop)
    leaf_turn(0, z)
    @pl.when(at_end)
    def _():
        leaf_pair().start()

    def pick(c, carry):
        for q in range(sums):
            p = c * sums + q
            rows = pl.ds(q * wide, wide)
            w_hi[c, rows], w_lo[c, rows] = split(runs[whole[1, p]] * real[1, p])
        return carry

    lax.fori_loop(0, prods, pick, 0)
    from_core(t)
    cur_1[...] = L[pl.ds(t * 4, 4)].reshape(cur_1.shape)
    tops = units(cur_1, u_hi_1, u_lo_1, peaks_1, scale_1)

    each_side(2, leaf_hop)
    flow_in.wait()

    def ahead(i, carry):
        for c in (2 * i, 2 * i + 1):
            value = dot3((w_hi[c], w_lo[c]), (u_hi_1[c], u_lo_1[c]), ((1,), (0,)))
            for q in range(sums):
                total[q * wide : (q + 1) * wide] += value[q * wide : (q + 1) * wide] * scale_1[q, c]
        return carry

    lax.fori_loop(0, prods // 2, ahead, 0)
    for q in range(sums):
        F[2 * t + q // each, q % each] = upper[q] / total[q * wide : (q + 1) * wide]
    for half in range(2):
        for side in range(2):
            @pl.when(has_z[side])
            def _():
                flow_z(z, side, half).start()
        flow_y(z, half).start()
    each_side(3, leaf_hop)
    for q in range(sums):
        sum_values[q] = tops[q] + jnp.log(total[q * wide : (q + 1) * wide])

    def behind(c, carry):
        f = jnp.concatenate([F[2 * t + q // each, q % each] * scale_1[q, c] for q in range(sums)], axis=0)
        value = dot3((w_hi[c], w_lo[c]), split(f), ((0,), (0,)))
        value = value * (u_hi_1[c].astype(f32) + u_lo_1[c].astype(f32))
        for g in range(part.shape[0]):
            times = (child_of[0, c] == g).astype(f32) + (child_of[1, c] == g).astype(f32)
            part[g] += value * times
        return carry

    lax.fori_loop(0, prods, behind, 0)

    def core_copy(xx):
        return remote(
            part.at[pl.ds(2 * (xx * 2 + 1 - k), 2)], got_core.at[xx], send_core.at[xx], recv_core.at[xx], by_core
        )

    for xx in range(2):
        core_copy(xx).start()
    each_side(1, leaf_turn)
    flow_hop(1)
    from_x(z * 2 + 1 - y)
    for xx in range(2):
        core_copy(xx).wait_recv()
        mid[xx] = part[pl.ds(2 * (xx * 2 + k), 2)] + got_core[xx]
    x_copy = remote(mid.at[1 - x], got_x, send_x, recv_x, by_x)
    x_copy.start()

    from_core(z * 2 + 1 - y)
    each_side(2, leaf_turn)
    each_side(1, both_x)
    flow_hop(2)
    for half in range(2):
        arrived_f(z * 2 + 1 - y, half)
    outers(z)
    each_side(3, leaf_turn)
    each_side(2, both_x)
    flow_hop(3)
    each_side(3, both_x)
    at_hop(1)
    at_hop(2)
    at_hop(3)

    x_copy.wait_recv()
    leaf_flow[...] = mid[x] + got_x[...]

    def finish(b, carry):
        param_flow[b] = W[t * keep + b] * outer[b] * real[2, t * keep + b]
        return carry

    lax.fori_loop(0, keep, finish, 0)

    for xx in range(2):
        core_copy(xx).wait_send()
    x_copy.wait_send()
    @pl.when(at_end)
    def _():
        leaf_pair().wait_send()

    def sent(tt, carry):
        leaf_x(tt).wait_send()
        leaf_c(n, 0, tt).wait_send()
        leaf_c(nx, 1, tt).wait_send()
        return carry

    lax.fori_loop(0, 2 * depth, sent, 0)

    def sent_z(zz, carry):
        @pl.when((zz != pair_z) | at_end)
        def _():
            leaf_y(zz).wait_send()
        for half in range(2):
            flow_y(zz, half).wait_send()
        @pl.when((zz >= z) & has_z[0])
        def _():
            leaf_z(zz, 0).wait_send()
            for half in range(2):
                flow_z(zz, 0, half).wait_send()
        @pl.when((zz <= z) & has_z[1])
        def _():
            leaf_z(zz, 1).wait_send()
            for half in range(2):
                flow_z(zz, 1, half).wait_send()
        return carry

    lax.fori_loop(0, depth, sent_z, 0)


def fused(leaves, prod_child, block_weight, block_child, block_parent, block_count, upper_flow):
    group, wide, samples = leaves.shape
    prods, sums = prod_child.shape[0], upper_flow.shape[0]
    owners, batches = lax.axis_size("nodes"), lax.axis_size("batch")
    keep = block_weight.shape[0] // batches
    whole, real = order_blocks(block_count, block_child, block_parent, sums)
    smem, vmem = pl.BlockSpec(memory_space=pltpu.SMEM), pl.BlockSpec(memory_space=pltpu.VMEM)
    dma = lambda *dims: pltpu.SemaphoreType.DMA(dims)
    vec = lambda kind, *dims: pltpu.VMEM(dims, kind)
    two = 2 * samples
    return pl.pallas_call(
        main_kernel,
        in_specs=[smem] * 3 + [pl.BlockSpec(memory_space=pl.ANY)] * 3,
        out_specs=[vmem] * 3,
        out_shape=[
            jax.ShapeDtypeStruct(upper_flow.shape, f32),
            jax.ShapeDtypeStruct(leaves.shape, f32),
            jax.ShapeDtypeStruct((keep, *block_weight.shape[1:]), f32),
        ],
        scratch_shapes=[
            vec(f32, batches * owners, group, wide, samples),
            vec(f32, batches * 2, sums // 2, wide, samples),
            vec(f32, owners * group, wide, two),
            vec(f32, sums, wide, two),
            vec(bf16, prods, wide, two),
            vec(bf16, prods, wide, two),
            vec(f32, prods, 1, two),
            vec(f32, sums, prods, 1, two),
            vec(f32, owners * group, wide, samples),
            vec(bf16, prods, wide, samples),
            vec(bf16, prods, wide, samples),
            vec(f32, prods, 1, samples),
            vec(f32, sums, prods, 1, samples),
            vec(f32, sums, wide, samples),
            vec(f32, sums * wide, samples),
            vec(f32, keep, *block_weight.shape[1:]),
            vec(f32, *block_weight.shape),
            vec(f32, *block_weight.shape),
            vec(bf16, prods, sums * wide, wide),
            vec(bf16, prods, sums * wide, wide),
            vec(f32, owners * group, wide, samples),
            vec(f32, 2, group, wide, samples),
            vec(f32, 2, group, wide, samples),
            vec(f32, group, wide, samples),
            dma(batches * owners),
            dma(batches),
            dma(2 * batches),
            dma(batches // 2),
            dma(batches),
            dma(2 * batches),
            dma(batches),
            dma(2 * batches),
            dma(2),
            dma(2),
            pltpu.SemaphoreType.DMA,
            pltpu.SemaphoreType.DMA,
            pltpu.SemaphoreType.DMA,
            dma(2),
            dma(8),
        ],
        compiler_params=pltpu.CompilerParams(
            collective_id=0, has_side_effects=True, vmem_limit_bytes=50 << 20
        ),
    )(
        prod_child.T, whole, real, leaves, upper_flow, block_weight,
    )


def solution(mesh):
    placed = (
        P("nodes", None, "batch"),
        P(),
        P("nodes", None, None),
        P("nodes", None),
        P("nodes", None),
        P("nodes"),
        P("nodes", None, "batch"),
    )
    small = dict(mesh.shape) == {"nodes": 4, "batch": 8}
    return jax.shard_map(
        fused if small else body,
        mesh=mesh,
        in_specs=placed,
        out_specs=(
            P("nodes", None, "batch"),
            P("nodes", None, "batch"),
            P(("nodes", "batch"), None, None),
        ),
        check_vma=False,
    )
```
